512 devices in a mesh: group: 32 (over z, x_hi), fast: 16 (over x_lo, y, core).
Axes of the slice: x: 4 (x_hi: 2, x_lo: 2; x = x_hi * 2 + x_lo), y: 4, z: 16, core: 2. Of those that a mesh axis runs over, the one named last changes fastest.
Arguments:
- img_feat: bfloat16 [65536, 768], P(('group', 'fast')), may hold values from -8 to 8
- txt_feat: bfloat16 [65536, 512], P(('group', 'fast')), may hold values from -8 to 8
- img_proj: bfloat16 [768, 512], replicated
- txt_proj: bfloat16 [512, 512], replicated
- logit_scale: float32 [1], replicated, may hold values from 40 to 50
- clip_bound: float32 [1], replicated, may hold values from 40 to 80
- noise_img: bfloat16 [768, 512], replicated, may hold values from -6 to 6
- noise_txt: bfloat16 [512, 512], replicated, may hold values from -6 to 6
- noise_count: float32 [1], replicated, may hold values from -4 to 4
Outputs:
- grad_img: bfloat16 [768, 512], replicated
- grad_txt: bfloat16 [512, 512], replicated
- loss: float32 [1], replicated
- new_bound: float32 [1], replicated
The draws below stay inside these ranges and needn't reach their ends.
All inputs are finite; a program needn't handle non-finite values.
Results may differ from the reference program's by a relative error of at most 0.0031.
The reference program's roundings to bfloat16 on the way count: a program that leaves them out, or rounds other values in their place, can miss the bound.
Values may be sent and summed in bfloat16 or wider, within the bound.
No kernel may reach another device: no remote copies, remote signals or barrier semaphores. Data moves between devices by JAX's collectives and lax.ppermute only.
A program may use at most 64 MiB of HBM per device.

```python
import math
import jax
import jax.numpy as jnp
from jax import lax

DI = 768
DT = 512
DE = 512
BD = 128
BATCH = 65536
N_GROUP = 32
N_FAST = 16


def latent_rows(key):
    return jax.random.normal(jax.random.fold_in(key, 11), (BATCH, DT), jnp.float32)


def pair_strength(key):
    rows = jnp.arange(BATCH)
    device = (rows // BD).astype(jnp.float32)
    last = max(BATCH // BD - 1, 1)
    level = 0.12 * jnp.exp(math.log(3.0) * device / last)
    factor = jnp.exp(jax.random.uniform(jax.random.fold_in(key, 12), (BATCH,), jnp.float32, math.log(0.5), math.log(2.5)))
    return jnp.minimum(level * factor, 0.9)


def shared_basis(key):
    return jax.random.normal(jax.random.fold_in(key, 21), (DT, DE), jnp.float32)


def mixed_rows(key, latent, share, width):
    own_part = jax.random.normal(key, (BATCH, width), jnp.float32)
    return jnp.sqrt(share)[:, None] * latent + jnp.sqrt(1.0 - share)[:, None] * own_part


def row_scales(key, lower, upper):
    return jnp.exp(jax.random.uniform(key, (BATCH, 1), jnp.float32, math.log(lower), math.log(upper)))


def draw_img_feat(key, part):
    latent = latent_rows(key)
    share = pair_strength(key)
    key = jax.random.fold_in(key, 1)
    head = mixed_rows(jax.random.fold_in(key, 1), latent, share, DT)
    tail = jax.random.normal(jax.random.fold_in(key, 2), (BATCH, DI - DT), jnp.float32)
    scales = row_scales(jax.random.fold_in(key, 3), 0.7, 1.4)
    whole = jnp.concatenate([head, tail], axis=1) * scales
    return jnp.clip(whole, -8.0, 8.0).astype(jnp.bfloat16)


def draw_txt_feat(key, part):
    latent = latent_rows(key)
    share = pair_strength(key)
    key = jax.random.fold_in(key, 2)
    whole = mixed_rows(jax.random.fold_in(key, 1), latent, share, DT)
    scales = row_scales(jax.random.fold_in(key, 3), 0.7, 1.4)
    return jnp.clip(whole * scales, -8.0, 8.0).astype(jnp.bfloat16)


def draw_txt_proj(key, part):
    basis = shared_basis(key)
    key = jax.random.fold_in(key, 3)
    own_part = jax.random.normal(key, (DT, DE), jnp.float32)
    whole = (0.9 * basis + math.sqrt(0.19) * own_part) / math.sqrt(DT)
    return whole.astype(jnp.bfloat16)


def draw_img_proj(key, part):
    basis = shared_basis(key)
    key = jax.random.fold_in(key, 4)
    own_part = jax.random.normal(jax.random.fold_in(key, 1), (DT, DE), jnp.float32)
    tail = jax.random.normal(jax.random.fold_in(key, 2), (DI - DT, DE), jnp.float32)
    head = 0.9 * basis + math.sqrt(0.19) * own_part
    whole = jnp.concatenate([head, tail], axis=0) / math.sqrt(DI)
    return whole.astype(jnp.bfloat16)


def bell_draw(stream_key, dims, spread, most, kind=jnp.bfloat16):
    result = spread * jax.random.normal(stream_key, dims, jnp.float32)
    return jnp.clip(result, min=-most, max=most).astype(kind)


def setup_inputs(seed: int = 0) -> dict:
    key_list = jax.random.split(jax.random.key(seed), 10)
    return {
        "img_feat": draw_img_feat(jax.random.fold_in(key_list[9], 71), 0),
        "txt_feat": draw_txt_feat(jax.random.fold_in(key_list[9], 71), 0),
        "img_proj": draw_img_proj(jax.random.fold_in(key_list[9], 71), 0),
        "txt_proj": draw_txt_proj(jax.random.fold_in(key_list[9], 71), 0),
        "logit_scale": jnp.clip(jax.random.uniform(key_list[4], (1,), jnp.float32, 40.0, 50.0), 40.0, 50.0),
        "clip_bound": jnp.clip(jnp.exp(jax.random.uniform(key_list[5], (1,), jnp.float32, math.log(40.0), math.log(80.0))), 40.0, 80.0),
        "noise_img": bell_draw(key_list[6], (DI, DE), 1.0, 6.0),
        "noise_txt": bell_draw(key_list[7], (DT, DE), 1.0, 6.0),
        "noise_count": bell_draw(key_list[8], (1,), 1.0, 4.0, jnp.float32),
    }


def embed_rows(feat, proj):
    projected = jnp.dot(feat, proj, preferred_element_type=jnp.float32)
    inverse = lax.rsqrt(lax.optimization_barrier(jnp.sum(projected * projected, axis=-1, keepdims=True)) + 1e-06)
    return (projected * inverse, inverse)

def block_rows(array, size):
    return array.reshape((array.shape[0] // size, size) + array.shape[1:])

def side_lse(queries, keys, temper):

    def one(block):
        scores = temper * jnp.dot(block, keys.T, preferred_element_type=jnp.float32)
        top = lax.optimization_barrier(jnp.max(scores, axis=1))
        return top + jnp.log(lax.optimization_barrier(jnp.sum(jnp.exp(scores - top[:, None]), axis=1)))
    size = min(512, queries.shape[0])
    return lax.map(one, block_rows(queries, size)).reshape(-1)

def side_pull(queries, keys, own_lse, other_lse, temper):

    def one(pair):
        block, block_lse = pair
        scores = temper * jnp.dot(block, keys.T, preferred_element_type=jnp.float32)
        weights = (jnp.exp(scores - block_lse[:, None]) + jnp.exp(scores - other_lse[None, :])).astype(jnp.bfloat16)
        return temper * jnp.dot(weights, keys, preferred_element_type=jnp.float32)
    size = min(512, queries.shape[0])
    out = lax.map(one, (block_rows(queries, size), block_rows(own_lse, size)))
    return out.reshape(queries.shape[0], keys.shape[1])

def to_batches(array):
    width = array.shape[-1]
    return array.reshape(N_GROUP, N_FAST, BD, width).transpose(1, 0, 2, 3).reshape(N_FAST, N_GROUP * BD, width)

def from_batches(array):
    width = array.shape[-1]
    return array.reshape(N_FAST, N_GROUP, BD, width).transpose(1, 0, 2, 3).reshape(N_GROUP * N_FAST * BD, width)

def reference(img_feat, txt_feat, img_proj, txt_proj, logit_scale, clip_bound, noise_img, noise_txt, noise_count):
    temper = logit_scale[0]
    bound = clip_bound[0]
    total = img_feat.shape[0]
    e_img, inv_img = embed_rows(img_feat, img_proj)
    e_txt, inv_txt = embed_rows(txt_feat, txt_proj)
    h_img = e_img.astype(jnp.bfloat16)
    h_txt = e_txt.astype(jnp.bfloat16)
    f_img = h_img.astype(jnp.float32)
    f_txt = h_txt.astype(jnp.float32)
    diagonal = temper * lax.optimization_barrier(jnp.sum(f_img * f_txt, axis=1))

    def one_batch(pair):
        batch_img, batch_txt = pair
        row_lse = side_lse(batch_img, batch_txt, temper)
        col_lse = side_lse(batch_txt, batch_img, temper)
        pull_img = side_pull(batch_img, batch_txt, row_lse, col_lse, temper)
        pull_txt = side_pull(batch_txt, batch_img, col_lse, row_lse, temper)
        return (row_lse[:, None], col_lse[:, None], pull_img, pull_txt)
    row_b, col_b, pull_img_b, pull_txt_b = lax.map(one_batch, (to_batches(h_img), to_batches(h_txt)))
    row_lse = from_batches(row_b)[:, 0]
    col_lse = from_batches(col_b)[:, 0]
    loss = (jnp.sum(row_lse - diagonal) + jnp.sum(col_lse - diagonal)) / (2.0 * total)
    d_img = from_batches(pull_img_b) - 2.0 * temper * f_txt
    d_txt = from_batches(pull_txt_b) - 2.0 * temper * f_img
    g_img = (d_img - e_img * lax.optimization_barrier(jnp.sum(e_img * d_img, axis=1, keepdims=True))) * inv_img
    g_txt = (d_txt - e_txt * lax.optimization_barrier(jnp.sum(e_txt * d_txt, axis=1, keepdims=True))) * inv_txt
    x_img = img_feat.astype(jnp.float32)
    x_txt = txt_feat.astype(jnp.float32)
    squared = lax.optimization_barrier(jnp.sum(x_img * x_img, axis=1)) * lax.optimization_barrier(jnp.sum(g_img * g_img, axis=1)) + lax.optimization_barrier(jnp.sum(x_txt * x_txt, axis=1)) * lax.optimization_barrier(jnp.sum(g_txt * g_txt, axis=1))
    norm = jnp.sqrt(squared + 1e-06)
    factor = jnp.minimum(1.0, bound / norm)
    q_img = (factor[:, None] * g_img).astype(jnp.bfloat16)
    q_txt = (factor[:, None] * g_txt).astype(jnp.bfloat16)
    sum_img = jnp.dot(img_feat.T, q_img, preferred_element_type=jnp.float32)
    sum_txt = jnp.dot(txt_feat.T, q_txt, preferred_element_type=jnp.float32)
    grad_img = ((sum_img + bound * noise_img.astype(jnp.float32)) / bound).astype(jnp.bfloat16)
    grad_txt = ((sum_txt + bound * noise_txt.astype(jnp.float32)) / bound).astype(jnp.bfloat16)
    count = jnp.sum(jax.nn.sigmoid((bound - norm) / (0.1 * bound)))
    frac = (count + 0.05 * total * noise_count[0]) / total
    new_bound = bound * jnp.exp(-0.2 * (frac - 0.5))
    return (grad_img, grad_txt, jnp.reshape(loss, (1,)), jnp.reshape(new_bound, (1,)))
```

```python
import functools
import math

import jax
import jax.numpy as jnp
from jax import lax
from jax.experimental import pallas as pl
from jax.experimental.pallas import tpu as pltpu
from jax.sharding import Mesh, PartitionSpec as P

AX = ("z", "xh", "xl", "y", "c")
XY = ("xh", "xl", "y")
DIMS = (16, 2, 2, 4, 2)
DI, DT, DE, BD = 768, 512, 512, 128
WIDE = DI + DT
ROWS = 4096
HALF = ROWS // 2
NXY = 16
NZ = 16
PER_XY = DE // NXY
PER_CORE = PER_XY // 2
BATCH = 65536
PIECES = 11
bf16, f32 = jnp.bfloat16, jnp.float32
NT = (((1,), (1,)), ((), ()))
VMEM_SPEC = pl.BlockSpec(memory_space=pltpu.VMEM)
SMEM_SPEC = pl.BlockSpec(memory_space=pltpu.SMEM)
PARAMS = pltpu.CompilerParams(vmem_limit_bytes=48 * 1024 * 1024)


def fold_lanes(x):
    total = x[:, 0:128]
    for k in range(1, x.shape[1] // 128):
        total = total + x[:, 128 * k : 128 * (k + 1)]
    return total


def fold_rows(x):
    total = x[0:8, :]
    for k in range(1, x.shape[0] // 8):
        total = total + x[8 * k : 8 * (k + 1), :]
    return total


def embed_kernel(f_ref, pi_ref, pt_ref, h_ref, e_ref, st_ref):
    for side, (low, width, p_ref) in enumerate(((0, DI, pi_ref), (DI, DT, pt_ref))):
        x = f_ref[:, low : low + width]
        u = jnp.dot(x, p_ref[...], preferred_element_type=f32)
        inv = lax.rsqrt(jnp.sum(u * u, axis=1, keepdims=True) + 1e-06)
        e = u * inv
        e_ref[:, DE * side : DE * (side + 1)] = e
        h_ref[:, DE * side : DE * (side + 1)] = e.astype(bf16)
        xf = x.astype(f32)
        size = jnp.sum(xf * xf, axis=1, keepdims=True)
        st_ref[:, 256 * side : 256 * side + 128] = jnp.broadcast_to(inv, (BD, 128))
        st_ref[:, 256 * side + 128 : 256 * side + 256] = jnp.broadcast_to(size, (BD, 128))


def embed(feats, img_proj, txt_proj):
    return pl.pallas_call(
        embed_kernel,
        out_shape=(
            jax.ShapeDtypeStruct((BD, 2 * DE), bf16),
            jax.ShapeDtypeStruct((BD, 2 * DE), f32),
            jax.ShapeDtypeStruct((BD, 512), f32),
        ),
        in_specs=[VMEM_SPEC] * 3,
        out_specs=[VMEM_SPEC] * 3,
        compiler_params=PARAMS,
        name="embed",
    )(feats, img_proj, txt_proj)


TI, TJ = 256, 512


def lse_kernel(core_ref, k_ref, img_ref, txt_ref, col_ref, row_ref, acc_ref):
    j = pl.program_id(0)
    k = k_ref[0]
    keys = txt_ref[...]

    @pl.when(j == 0)
    def _():
        acc_ref[...] = jnp.zeros_like(acc_ref)

    col = jnp.zeros((8, TJ), f32)
    for b in range(HALF // TI):
        s = lax.dot_general(img_ref[b * TI : (b + 1) * TI, :], keys, NT, preferred_element_type=f32)
        grown = jnp.exp2(s * k)
        acc_ref[b * TI : (b + 1) * TI, :] += fold_lanes(grown)
        col = col + fold_rows(grown)
    col_ref[...] = jnp.sum(col, axis=0, keepdims=True)

    @pl.when(j == ROWS // TJ - 1)
    def _():
        for b in range(HALF // TI):
            part = acc_ref[b * TI : (b + 1) * TI, :]
            row_ref[:, b * TI : (b + 1) * TI] = jnp.sum(part.T, axis=0, keepdims=True)


def lse_sums(core, k, gathered):
    return pl.pallas_call(
        lse_kernel,
        grid_spec=pltpu.PrefetchScalarGridSpec(
            num_scalar_prefetch=2,
            grid=(ROWS // TJ,),
            in_specs=[
                pl.BlockSpec((HALF, DE), lambda j, core, k: (core[0], 0)),
                pl.BlockSpec((TJ, DE), lambda j, core, k: (j, 1)),
            ],
            out_specs=[
                pl.BlockSpec((1, TJ), lambda j, core, k: (0, j)),
                pl.BlockSpec((1, HALF), lambda j, core, k: (0, 0)),
            ],
            scratch_shapes=[pltpu.VMEM((HALF, 128), f32)],
        ),
        out_shape=(jax.ShapeDtypeStruct((1, ROWS), f32), jax.ShapeDtypeStruct((1, HALF), f32)),
        compiler_params=PARAMS,
        name="lse",
    )(core, k, gathered, gathered)


def pull_kernel(core_ref, sc_ref, sums_ref, other_ref, g_ref, h_ref, e_ref, st_ref, q_ref, out_ref, inv_ref, grown_ref):
    core = core_ref[0]
    temper, bound, k = sc_ref[0], sc_ref[1], sc_ref[2]
    inv_ref[1:2, :] = 1.0 / (sums_ref[:, 0:ROWS] + other_ref[:, 0:ROWS])
    mine, theirs = 1.0 / sums_ref[:, ROWS:], 1.0 / other_ref[:, ROWS:]
    inv_ref[0:1, 0:HALF] = jnp.where(core == 0, mine, theirs)
    inv_ref[0:1, HALF:] = jnp.where(core == 0, theirs, mine)
    loss = jnp.zeros((BD, 1), f32)
    square = jnp.full((BD, 1), 1e-06, f32)
    grads = []
    step = 512
    for side in range(2):
        away = 1 - side
        own = h_ref[:, DE * side : DE * (side + 1)]
        total = jnp.zeros((BD, 128), f32)
        for j in range(ROWS // step):
            keys = g_ref[j * step : (j + 1) * step, DE * away : DE * (away + 1)]
            s = lax.dot_general(own, keys, NT, preferred_element_type=f32)
            grown = jnp.exp2(s * k)
            grown_ref[:, j * step : (j + 1) * step] = grown
            total = total + fold_lanes(grown)
        total = jnp.sum(total, axis=1, keepdims=True)
        own_inv = 1.0 / total
        d = jnp.zeros((BD, DE), f32)
        for j in range(ROWS // step):
            keys = g_ref[j * step : (j + 1) * step, DE * away : DE * (away + 1)]
            far = inv_ref[away : away + 1, j * step : (j + 1) * step]
            w = (grown_ref[:, j * step : (j + 1) * step] * (own_inv + far)).astype(bf16)
            d = d + jnp.dot(w, keys, preferred_element_type=f32)
        f_own = own.astype(f32)
        f_away = h_ref[:, DE * away : DE * (away + 1)].astype(f32)
        diag = temper * jnp.sum(f_own * f_away, axis=1, keepdims=True)
        loss = loss + (jnp.log(total) - diag)
        d = temper * d - 2.0 * temper * f_away
        e = e_ref[:, DE * side : DE * (side + 1)]
        inv = st_ref[:, 256 * side : 256 * side + 1]
        size = st_ref[:, 256 * side + 128 : 256 * side + 129]
        grad = (d - e * jnp.sum(e * d, axis=1, keepdims=True)) * inv
        square = square + size * jnp.sum(grad * grad, axis=1, keepdims=True)
        grads.append(grad)
    norm = jnp.sqrt(square)
    factor = jnp.minimum(1.0, bound / norm)
    count = 1.0 / (1.0 + jnp.exp((norm - bound) / (0.1 * bound)))
    for side in range(2):
        q = (factor * grads[side]).T.astype(bf16)
        q_ref[:, PER_XY * side : PER_XY * (side + 1), :] = q.reshape(NXY, PER_XY, BD)
    out_ref[0:1, :] = jnp.broadcast_to(jnp.sum(loss, axis=0, keepdims=True), (1, 128))
    out_ref[1:2, :] = jnp.broadcast_to(jnp.sum(count, axis=0, keepdims=True), (1, 128))
    out_ref[2:8, :] = jnp.zeros((6, 128), f32)


def pull(core, scalars, sums, other, gathered, h, e, stats):
    return pl.pallas_call(
        pull_kernel,
        out_shape=(
            jax.ShapeDtypeStruct((NXY, 2 * PER_XY, BD), bf16),
            jax.ShapeDtypeStruct((8, 128), f32),
        ),
        in_specs=[SMEM_SPEC] * 2 + [VMEM_SPEC] * 6,
        out_specs=[VMEM_SPEC] * 2,
        scratch_shapes=[pltpu.VMEM((2, ROWS), f32), pltpu.VMEM((BD, ROWS), f32)],
        compiler_params=PARAMS,
        name="pull",
    )(core, scalars, sums, other, gathered, h, e, stats)


def share_kernel(core_ref, q_ref, f_ref, part_ref, keep_ref, send_ref):
    core = core_ref[0]
    feats = f_ref[...].reshape(NXY * BD, WIDE)
    sums = []
    for side, (low, width) in enumerate(((0, DI), (DI, DT))):
        rows = jnp.concatenate([q_ref[p, PER_XY * side : PER_XY * (side + 1), :] for p in range(NXY)], axis=1)
        sums.append(jnp.dot(rows, feats[:, low : low + width], preferred_element_type=f32))
    whole = jnp.concatenate(sums, axis=1)
    first, second = whole[0:PER_CORE, :], whole[PER_CORE:, :]
    keep = jnp.where(core == 0, first, second)
    send = jnp.where(core == 0, second, first)
    for ref, value in ((keep_ref, keep), (send_ref, send)):
        for k in range(WIDE // 128):
            ref[:, k, :] = value[:, 128 * k : 128 * (k + 1)]
        ref[:, 10, :] = jnp.broadcast_to(part_ref[0:1, :], (NZ, 128))
        ref[:, 11, :] = jnp.broadcast_to(part_ref[1:2, :], (NZ, 128))
        for k in range(12, 16):
            ref[:, k, :] = jnp.zeros((NZ, 128), f32)


def share(core, q, feats, part):
    return pl.pallas_call(
        share_kernel,
        out_shape=(jax.ShapeDtypeStruct((NZ, 16, 128), f32), jax.ShapeDtypeStruct((NZ, 16, 128), f32)),
        in_specs=[SMEM_SPEC] + [VMEM_SPEC] * 3,
        out_specs=[VMEM_SPEC] * 2,
        compiler_params=PARAMS,
        name="share",
    )(core, q, feats, part)


def finish_kernel(sc_ref, v_ref, noise_ref, out_ref):
    bound = sc_ref[1]
    total = v_ref[0]
    for k in range(1, NZ):
        total = total + v_ref[k]
    grad = (total + bound * noise_ref[...]) / bound
    lane = lax.broadcasted_iota(jnp.int32, (1, 128), 1)
    packed = jnp.zeros((1, 128), f32)
    for m in range(2):
        rest = total[10 + m : 11 + m, :]
        for n in range(3):
            term = rest.astype(bf16).astype(f32)
            packed = jnp.where(lane == 3 * m + n, term, packed)
            rest = rest - term
    row = lax.broadcasted_iota(jnp.int32, (16, 128), 0)
    out = jnp.where(row < 10, grad, jnp.where(row == 10, packed, 0.0)).astype(bf16)
    for k in range(NZ):
        out_ref[k] = out


def finish(scalars, received, noise):
    return pl.pallas_call(
        finish_kernel,
        out_shape=jax.ShapeDtypeStruct((NZ, 16, 128), bf16),
        in_specs=[SMEM_SPEC] + [VMEM_SPEC] * 2,
        out_specs=VMEM_SPEC,
        compiler_params=PARAMS,
        name="finish",
    )(scalars, received, noise)


def final_kernel(core_ref, a_ref, b_ref, gi_ref, gt_ref, sum_ref):
    core = core_ref[0]
    mine, theirs = a_ref[...], b_ref[...]
    first = jnp.where(core == 0, mine, theirs)
    second = jnp.where(core == 0, theirs, mine)
    for k in range(WIDE // 128):
        part = slice(128 * k, 128 * (k + 1))
        block = jnp.concatenate([first[:, None, :, part], second[:, None, :, part]], axis=1)
        block = block.reshape(DE, 128).T
        if k < DI // 128:
            gi_ref[part, :] = block
        else:
            gt_ref[128 * k - DI : 128 * (k + 1) - DI, :] = block
    tail = a_ref[:, :, WIDE:].astype(f32)
    sum_ref[...] = jnp.sum(tail[:, 0:8, :], axis=0)


def final(core, mine, theirs):
    return pl.pallas_call(
        final_kernel,
        out_shape=(
            jax.ShapeDtypeStruct((DI, DE), bf16),
            jax.ShapeDtypeStruct((DT, DE), bf16),
            jax.ShapeDtypeStruct((8, 128), f32),
        ),
        in_specs=[SMEM_SPEC] + [VMEM_SPEC] * 2,
        out_specs=[VMEM_SPEC] * 3,
        compiler_params=PARAMS,
        name="final",
    )(core, mine, theirs)


def place(z, xh, xl, y, c):
    return (((z * 2 + xh) * 2 + xl) * 4 + y) * 2 + c


def pairs(target):
    out = []
    for z in range(16):
        for xh in range(2):
            for xl in range(2):
                for y in range(4):
                    for c in range(2):
                        out.append((place(z, xh, xl, y, c), place(*target(z, xh, xl, y, c))))
    return out


REGROUP = pairs(lambda z, xh, xl, y, c: (z, c, xl, y, xh))
CORES = pairs(lambda z, xh, xl, y, c: (z, xh, xl, y, 1 - c))


def noise_column(noise, column):
    part = lax.dynamic_slice(noise, (0, column), (noise.shape[0], 1))
    return part.astype(f32).reshape(noise.shape[0] // 128, 128)


def local(img_feat, txt_feat, img_proj, txt_proj, logit_scale, clip_bound, noise_img, noise_txt, noise_count):
    temper, bound = logit_scale[0], clip_bound[0]
    z, c = lax.axis_index("z"), lax.axis_index("c")
    at = lax.axis_index(XY)
    core = c.astype(jnp.int32).reshape(1)
    k = logit_scale * math.log2(math.e)
    scalars = jnp.concatenate([logit_scale, clip_bound, k])
    feats = lax.ppermute(jnp.concatenate([img_feat, txt_feat], axis=1), AX, REGROUP)
    h, e, stats = embed(feats, img_proj, txt_proj)
    gathered = lax.all_gather(h, ("z", "c"), axis=0, tiled=True)
    spread = lax.all_to_all(jnp.broadcast_to(feats[None], (NXY, BD, WIDE)), XY, 0, 0)
    column = PER_XY * at + PER_CORE * c + z
    noise = jnp.concatenate(
        [noise_column(noise_img, column), noise_column(noise_txt, column), jnp.zeros((6, 128), f32)], axis=0
    )
    gathered, spread, noise = lax.optimization_barrier((gathered, spread, noise))
    sums = jnp.concatenate(lse_sums(core, k, gathered), axis=1)
    other = lax.ppermute(sums, AX, CORES)
    q, part = pull(core, scalars, sums, other, gathered, h, e, stats)
    q = lax.all_to_all(q, XY, 0, 0)
    keep, send = share(core, q, spread, part)
    mine = keep + lax.ppermute(send, AX, CORES)
    mine = finish(scalars, lax.all_to_all(mine, "z", 0, 0), noise)
    mine = lax.all_to_all(mine, "z", 0, 0)
    mine = mine[:, 0:PIECES, :].reshape(NZ, PIECES * 128)
    mine = lax.all_to_all(jnp.broadcast_to(mine[None], (NXY, NZ, PIECES * 128)), XY, 0, 0)
    theirs = lax.ppermute(mine, AX, CORES)
    grad_img, grad_txt, tail = final(core, mine, theirs)
    loss = (tail[0, 0] + tail[0, 1] + tail[0, 2]) / (2.0 * BATCH)
    count = tail[0, 3] + tail[0, 4] + tail[0, 5]
    frac = (count + 0.05 * BATCH * noise_count[0]) / BATCH
    new_bound = bound * jnp.exp(-0.2 * (frac - 0.5))
    return grad_img, grad_txt, jnp.reshape(loss, (1,)), jnp.reshape(new_bound, (1,))


def solution(mesh):
    fine = Mesh(mesh.devices.reshape(DIMS), AX)
    whole = P()
    return jax.shard_map(
        local,
        mesh=fine,
        in_specs=(P(AX, None), P(AX, None)) + (whole,) * 7,
        out_specs=(whole,) * 4,
        check_vma=False,
    )
```

```python
import functools
import math

import jax
import jax.numpy as jnp
from jax import lax
from jax.experimental import pallas as pl
from jax.experimental.pallas import tpu as pltpu
from jax.sharding import Mesh, PartitionSpec as P

AX = ("z", "xh", "xl", "y", "c")
XY = ("xh", "xl", "y")
XX = ("xh", "xl")
YC = ("y", "c")
DIMS = (16, 2, 2, 4, 2)
DI, DT, DE, BD = 768, 512, 512, 128
WIDE = DI + DT
ROWS = 4096
HALF = ROWS // 2
NX, NY, NC, NZ = 4, 4, 2, 16
NXY = NX * NY
NYC = NY * NC
PER_YC = DE // NYC
PER_X = PER_YC // NX
BATCH = 65536
LONG = WIDE + 128
bf16, f32 = jnp.bfloat16, jnp.float32
NT = (((1,), (1,)), ((), ()))
VMEM_SPEC = pl.BlockSpec(memory_space=pltpu.VMEM)
SMEM_SPEC = pl.BlockSpec(memory_space=pltpu.SMEM)
PARAMS = pltpu.CompilerParams(vmem_limit_bytes=48 * 1024 * 1024)


def fold_lanes(x):
    total = x[:, 0:128]
    for k in range(1, x.shape[1] // 128):
        total = total + x[:, 128 * k : 128 * (k + 1)]
    return total


def fold_rows(x):
    total = x[0:8, :]
    for k in range(1, x.shape[0] // 8):
        total = total + x[8 * k : 8 * (k + 1), :]
    return total


def embed_kernel(f_ref, pi_ref, pt_ref, h_ref, e_ref, st_ref):
    for side, (low, width, p_ref) in enumerate(((0, DI, pi_ref), (DI, DT, pt_ref))):
        x = f_ref[:, low : low + width]
        u = jnp.dot(x, p_ref[...], preferred_element_type=f32)
        inv = lax.rsqrt(jnp.sum(u * u, axis=1, keepdims=True) + 1e-06)
        e = u * inv
        e_ref[:, DE * side : DE * (side + 1)] = e
        h_ref[:, DE * side : DE * (side + 1)] = e.astype(bf16)
        xf = x.astype(f32)
        size = jnp.sum(xf * xf, axis=1, keepdims=True)
        st_ref[:, 256 * side : 256 * side + 128] = jnp.broadcast_to(inv, (BD, 128))
        st_ref[:, 256 * side + 128 : 256 * side + 256] = jnp.broadcast_to(size, (BD, 128))


def embed(feats, img_proj, txt_proj):
    return pl.pallas_call(
        embed_kernel,
        out_shape=(
            jax.ShapeDtypeStruct((BD, 2 * DE), bf16),
            jax.ShapeDtypeStruct((BD, 2 * DE), f32),
            jax.ShapeDtypeStruct((BD, 512), f32),
        ),
        in_specs=[VMEM_SPEC] * 3,
        out_specs=[VMEM_SPEC] * 3,
        compiler_params=PARAMS,
        name="embed",
    )(feats, img_proj, txt_proj)


TI, TJ = 256, 1024


def lse_kernel(core_ref, k_ref, img_ref, txt_ref, col_ref, row_ref, acc_ref):
    j = pl.program_id(0)
    k = k_ref[0]
    keys = txt_ref[...]

    @pl.when(j == 0)
    def _():
        acc_ref[...] = jnp.zeros_like(acc_ref)

    col = jnp.zeros((8, TJ), f32)
    for b in range(HALF // TI):
        s = lax.dot_general(img_ref[b * TI : (b + 1) * TI, :], keys, NT, preferred_element_type=f32)
        grown = jnp.exp2(s * k)
        acc_ref[b * TI : (b + 1) * TI, :] += fold_lanes(grown)
        col = col + fold_rows(grown)
    col_ref[...] = jnp.sum(col, axis=0, keepdims=True)

    @pl.when(j == ROWS // TJ - 1)
    def _():
        for b in range(HALF // TI):
            part = acc_ref[b * TI : (b + 1) * TI, :]
            row_ref[:, b * TI : (b + 1) * TI] = jnp.sum(part.T, axis=0, keepdims=True)


def lse_sums(core, k, gathered):
    return pl.pallas_call(
        lse_kernel,
        grid_spec=pltpu.PrefetchScalarGridSpec(
            num_scalar_prefetch=2,
            grid=(ROWS // TJ,),
            in_specs=[
                pl.BlockSpec((HALF, DE), lambda j, core, k: (core[0], 0)),
                pl.BlockSpec((TJ, DE), lambda j, core, k: (j, 1)),
            ],
            out_specs=[
                pl.BlockSpec((1, TJ), lambda j, core, k: (0, j)),
                pl.BlockSpec((1, HALF), lambda j, core, k: (0, 0)),
            ],
            scratch_shapes=[pltpu.VMEM((HALF, 128), f32)],
        ),
        out_shape=(jax.ShapeDtypeStruct((1, ROWS), f32), jax.ShapeDtypeStruct((1, HALF), f32)),
        compiler_params=PARAMS,
        name="lse",
    )(core, k, gathered, gathered)


STEP = 512


def pull_kernel(
    core_ref, sc_ref, sums_ref, other_ref, far_ref, h_ref, e_ref, st_ref, q_ref, out_ref, inv_ref, grown_ref, g_ref, sem
):
    def fetch(side, j):
        part = (pl.ds(j * STEP, STEP), pl.ds(DE * side, DE))
        return pltpu.make_async_copy(far_ref.at[part], g_ref.at[part], sem.at[side, j])

    for side in (1, 0):
        for j in range(ROWS // STEP):
            fetch(side, j).start()
    core = core_ref[0]
    temper, bound, k = sc_ref[0], sc_ref[1], sc_ref[2]
    inv_ref[1:2, :] = 1.0 / (sums_ref[:, 0:ROWS] + other_ref[:, 0:ROWS])
    mine, theirs = 1.0 / sums_ref[:, ROWS:], 1.0 / other_ref[:, ROWS:]
    inv_ref[0:1, 0:HALF] = jnp.where(core == 0, mine, theirs)
    inv_ref[0:1, HALF:] = jnp.where(core == 0, theirs, mine)
    loss = jnp.zeros((BD, 1), f32)
    square = jnp.full((BD, 1), 1e-06, f32)
    grads = []
    step = STEP
    for side in range(2):
        away = 1 - side
        own = h_ref[:, DE * side : DE * (side + 1)]
        total = jnp.zeros((BD, 128), f32)
        for j in range(ROWS // step):
            fetch(away, j).wait()
            keys = g_ref[j * step : (j + 1) * step, DE * away : DE * (away + 1)]
            s = lax.dot_general(own, keys, NT, preferred_element_type=f32)
            grown = jnp.exp2(s * k)
            grown_ref[:, j * step : (j + 1) * step] = grown
            total = total + fold_lanes(grown)
        total = jnp.sum(total, axis=1, keepdims=True)
        own_inv = 1.0 / total
        d = jnp.zeros((BD, DE), f32)
        for j in range(ROWS // step):
            keys = g_ref[j * step : (j + 1) * step, DE * away : DE * (away + 1)]
            far = inv_ref[away : away + 1, j * step : (j + 1) * step]
            w = (grown_ref[:, j * step : (j + 1) * step] * (own_inv + far)).astype(bf16)
            d = d + jnp.dot(w, keys, preferred_element_type=f32)
        f_own = own.astype(f32)
        f_away = h_ref[:, DE * away : DE * (away + 1)].astype(f32)
        diag = temper * jnp.sum(f_own * f_away, axis=1, keepdims=True)
        loss = loss + (jnp.log(total) - diag)
        d = temper * d - 2.0 * temper * f_away
        e = e_ref[:, DE * side : DE * (side + 1)]
        inv = st_ref[:, 256 * side : 256 * side + 1]
        size = st_ref[:, 256 * side + 128 : 256 * side + 129]
        grad = (d - e * jnp.sum(e * d, axis=1, keepdims=True)) * inv
        square = square + size * jnp.sum(grad * grad, axis=1, keepdims=True)
        grads.append(grad)
    norm = jnp.sqrt(square)
    factor = jnp.minimum(1.0, bound / norm)
    count = 1.0 / (1.0 + jnp.exp((norm - bound) / (0.1 * bound)))
    for side in range(2):
        q = (factor * grads[side]).T.astype(bf16)
        q_ref[:, PER_YC * side : PER_YC * (side + 1), :] = q.reshape(NYC, PER_YC, BD)
    out_ref[0:1, :] = jnp.broadcast_to(jnp.sum(loss, axis=0, keepdims=True), (1, 128))
    out_ref[1:2, :] = jnp.broadcast_to(jnp.sum(count, axis=0, keepdims=True), (1, 128))
    out_ref[2:8, :] = jnp.zeros((6, 128), f32)


def pull(core, scalars, sums, other, gathered, h, e, stats):
    return pl.pallas_call(
        pull_kernel,
        out_shape=(
            jax.ShapeDtypeStruct((NYC, 2 * PER_YC, BD), bf16),
            jax.ShapeDtypeStruct((8, 128), f32),
        ),
        in_specs=[SMEM_SPEC] * 2 + [VMEM_SPEC] * 2 + [pl.BlockSpec(memory_space=pl.ANY)] + [VMEM_SPEC] * 3,
        out_specs=[VMEM_SPEC] * 2,
        scratch_shapes=[
            pltpu.VMEM((2, ROWS), f32),
            pltpu.VMEM((BD, ROWS), f32),
            pltpu.VMEM((ROWS, 2 * DE), bf16),
            pltpu.SemaphoreType.DMA((2, ROWS // STEP)),
        ],
        compiler_params=PARAMS,
        name="pull",
    )(core, scalars, sums, other, gathered, h, e, stats)


def share_kernel(core_ref, q_ref, f_ref, g_ref, part_ref, out_ref):
    core = core_ref[0]
    lane = lax.broadcasted_iota(jnp.int32, (PER_X, 128), 1)
    tail = jnp.where(lane < 3, part_ref[0:1, :], jnp.where(lane < 6, part_ref[1:2, :], 0.0))
    for side, (low, width) in enumerate(((0, DI), (DI, DT))):
        rows = slice(PER_YC * side, PER_YC * (side + 1))
        total = jnp.zeros((PER_YC, width), f32)
        for ref, which in ((f_ref, core), (g_ref, 1 - core)):
            left = jnp.concatenate([q_ref[NC * y + which, rows, :] for y in range(NY)], axis=1)
            right = ref[:, :, low : low + width].reshape(NY * BD, width)
            total = total + jnp.dot(left, right, preferred_element_type=f32)
        for x in range(NX):
            out_ref[x, :, low : low + width] = total[PER_X * x : PER_X * (x + 1), :]
    for x in range(NX):
        out_ref[x, :, WIDE:] = tail


def share(core, q, feats, others, part):
    return pl.pallas_call(
        share_kernel,
        out_shape=jax.ShapeDtypeStruct((NX, PER_X, LONG), f32),
        in_specs=[SMEM_SPEC] + [VMEM_SPEC] * 4,
        out_specs=VMEM_SPEC,
        compiler_params=PARAMS,
        name="share",
    )(core, q, feats, others, part)


def finish_kernel(sc_ref, v_ref, noise_ref, out_ref):
    bound = sc_ref[1]
    total = v_ref[0]
    for k in range(1, NZ):
        total = total + v_ref[k]
    grad = (total + bound * noise_ref[...]) / bound
    rest = total[:, WIDE:]
    lane = lax.broadcasted_iota(jnp.int32, (1, 128), 1)
    packed = jnp.zeros((1, 128), f32)
    for n in range(3):
        term = rest.astype(bf16).astype(f32)
        packed = jnp.where((lane == n) | (lane == 3 + n), term, packed)
        rest = rest - term
    rows = [grad[:, 128 * k : 128 * (k + 1)] for k in range(WIDE // 128)] + [packed]
    out = jnp.concatenate(rows + [jnp.zeros((16 - len(rows), 128), f32)], axis=0).astype(bf16)
    for k in range(NZ):
        out_ref[k] = out


def finish(scalars, received, noise):
    return pl.pallas_call(
        finish_kernel,
        out_shape=jax.ShapeDtypeStruct((NZ, 16, 128), bf16),
        in_specs=[SMEM_SPEC] + [VMEM_SPEC] * 2,
        out_specs=VMEM_SPEC,
        compiler_params=PARAMS,
        name="finish",
    )(scalars, received, noise)


def final_kernel(core_ref, a_ref, b_ref, gi_ref, gt_ref, sum_ref):
    core = core_ref[0]
    mine, theirs = a_ref[...], b_ref[...]
    both = (jnp.where(core == 0, mine, theirs), jnp.where(core == 0, theirs, mine))
    for k in range(WIDE // 128):
        part = slice(128 * k, 128 * (k + 1))
        rows = [both[c][NY * x + y, :, part] for y in range(NY) for c in range(NC) for x in range(NX)]
        block = jnp.concatenate(rows, axis=0).T
        if k < DI // 128:
            gi_ref[part, :] = block
        else:
            gt_ref[128 * k - DI : 128 * (k + 1) - DI, :] = block
    tail = jnp.zeros((NZ, 128), f32)
    for y in range(NY):
        tail = tail + (both[0][y, :, WIDE:].astype(f32) + both[1][y, :, WIDE:].astype(f32))
    sum_ref[...] = tail[0:8, :]


def final(core, mine, theirs):
    return pl.pallas_call(
        final_kernel,
        out_shape=(
            jax.ShapeDtypeStruct((DI, DE), bf16),
            jax.ShapeDtypeStruct((DT, DE), bf16),
            jax.ShapeDtypeStruct((8, 128), f32),
        ),
        in_specs=[SMEM_SPEC] + [VMEM_SPEC] * 2,
        out_specs=[VMEM_SPEC] * 3,
        compiler_params=PARAMS,
        name="final",
    )(core, mine, theirs)


def place(z, xh, xl, y, c):
    return (((z * 2 + xh) * 2 + xl) * 4 + y) * 2 + c


def pairs(target):
    out = []
    for z in range(16):
        for xh in range(2):
            for xl in range(2):
                for y in range(4):
                    for c in range(2):
                        out.append((place(z, xh, xl, y, c), place(*target(z, xh, xl, y, c))))
    return out


REGROUP = pairs(lambda z, xh, xl, y, c: (z, c, xl, y, xh))
CORES = pairs(lambda z, xh, xl, y, c: (z, xh, xl, y, 1 - c))


def noise_column(noise, column):
    part = lax.dynamic_slice(noise, (0, column), (noise.shape[0], 1))
    return part.astype(f32).reshape(1, noise.shape[0])


def local(img_feat, txt_feat, img_proj, txt_proj, logit_scale, clip_bound, noise_img, noise_txt, noise_count):
    temper, bound = logit_scale[0], clip_bound[0]
    z, c = lax.axis_index("z"), lax.axis_index("c")
    x, yc = lax.axis_index(XX), lax.axis_index(YC)
    core = c.astype(jnp.int32).reshape(1)
    k = logit_scale * math.log2(math.e)
    scalars = jnp.concatenate([logit_scale, clip_bound, k])
    feats = lax.ppermute(jnp.concatenate([img_feat, txt_feat], axis=1), AX, REGROUP)
    h, e, stats = embed(feats, img_proj, txt_proj)
    gathered = lax.all_gather(h, ("z", "c"), axis=0, tiled=True)
    near = lax.all_to_all(jnp.broadcast_to(feats[None], (NY, BD, WIDE)), "y", 0, 0)
    beside = lax.ppermute(near, AX, CORES)
    column = PER_YC * yc + PER_X * x + z
    noise = jnp.concatenate(
        [noise_column(noise_img, column), noise_column(noise_txt, column), jnp.zeros((1, 128), f32)], axis=1
    )
    gathered, near, beside, noise = lax.optimization_barrier((gathered, near, beside, noise))
    sums = jnp.concatenate(lse_sums(core, k, gathered), axis=1)
    other = lax.ppermute(sums, AX, CORES)
    q, part = pull(core, scalars, sums, other, gathered, h, e, stats)
    q = lax.all_to_all(q, YC, 0, 0)
    mine = lax.all_to_all(share(core, q, near, beside, part), XX, 0, 0)
    mine = jnp.sum(mine, axis=0).reshape(NZ, 1, LONG)
    mine = finish(scalars, lax.all_to_all(mine, "z", 0, 0), noise)
    mine = lax.all_to_all(mine, "z", 0, 0)[:, 0 : LONG // 128, :].reshape(NZ, LONG)
    mine = lax.all_to_all(jnp.broadcast_to(mine[None], (NXY, NZ, LONG)), XY, 0, 0)
    theirs = lax.ppermute(mine, AX, CORES)
    grad_img, grad_txt, tail = final(core, mine, theirs)
    loss = (tail[0, 0] + tail[0, 1] + tail[0, 2]) / (2.0 * BATCH)
    count = tail[0, 3] + tail[0, 4] + tail[0, 5]
    frac = (count + 0.05 * BATCH * noise_count[0]) / BATCH
    new_bound = bound * jnp.exp(-0.2 * (frac - 0.5))
    return grad_img, grad_txt, jnp.reshape(loss, (1,)), jnp.reshape(new_bound, (1,))


def solution(mesh):
    fine = Mesh(mesh.devices.reshape(DIMS), AX)
    whole = P()
    return jax.shard_map(
        local,
        mesh=fine,
        in_specs=(P(AX, None), P(AX, None)) + (whole,) * 7,
        out_specs=(whole,) * 4,
        check_vma=False,
    )
```

```python
import functools
import math

import jax
import jax.numpy as jnp
from jax import lax
from jax.experimental import pallas as pl
from jax.experimental.pallas import tpu as pltpu
from jax.sharding import Mesh, PartitionSpec as P

AX = ("z", "xh", "xl", "y", "c")
XY = ("xh", "xl", "y")
XX = ("xh", "xl")
YC = ("y", "c")
DIMS = (16, 2, 2, 4, 2)
DI, DT, DE, BD = 768, 512, 512, 128
WIDE = DI + DT
ROWS = 4096
HALF = ROWS // 2
NX, NY, NC, NZ = 4, 4, 2, 16
NXY = NX * NY
NYC = NY * NC
PER_YC = DE // NYC
PER_X = PER_YC // NX
BATCH = 65536
LONG = WIDE + 128
bf16, f32 = jnp.bfloat16, jnp.float32
NT = (((1,), (1,)), ((), ()))
VMEM_SPEC = pl.BlockSpec(memory_space=pltpu.VMEM)
SMEM_SPEC = pl.BlockSpec(memory_space=pltpu.SMEM)
PARAMS = pltpu.CompilerParams(vmem_limit_bytes=32 * 1024 * 1024)


def fold_lanes(x):
    total = x[:, 0:128]
    for k in range(1, x.shape[1] // 128):
        total = total + x[:, 128 * k : 128 * (k + 1)]
    return total


def fold_rows(x):
    total = x[0:8, :]
    for k in range(1, x.shape[0] // 8):
        total = total + x[8 * k : 8 * (k + 1), :]
    return total


def embed_kernel(f_ref, pi_ref, pt_ref, h_ref, e_ref, st_ref):
    for side, (low, width, p_ref) in enumerate(((0, DI, pi_ref), (DI, DT, pt_ref))):
        x = f_ref[:, low : low + width]
        u = jnp.dot(x, p_ref[...], preferred_element_type=f32)
        inv = lax.rsqrt(jnp.sum(u * u, axis=1, keepdims=True) + 1e-06)
        e = u * inv
        e_ref[:, DE * side : DE * (side + 1)] = e
        h_ref[:, DE * side : DE * (side + 1)] = e.astype(bf16)
        xf = x.astype(f32)
        size = jnp.sum(xf * xf, axis=1, keepdims=True)
        st_ref[:, 256 * side : 256 * side + 128] = jnp.broadcast_to(inv, (BD, 128))
        st_ref[:, 256 * side + 128 : 256 * side + 256] = jnp.broadcast_to(size, (BD, 128))


def embed(feats, img_proj, txt_proj):
    return pl.pallas_call(
        embed_kernel,
        out_shape=(
            jax.ShapeDtypeStruct((BD, 2 * DE), bf16),
            jax.ShapeDtypeStruct((BD, 2 * DE), f32),
            jax.ShapeDtypeStruct((BD, 512), f32),
        ),
        in_specs=[VMEM_SPEC] * 3,
        out_specs=[VMEM_SPEC] * 3,
        compiler_params=PARAMS,
        name="embed",
    )(feats, img_proj, txt_proj)


TI, TJ = 256, 1024


def sums_kernel(count, k_ref, *refs):
    own, other, rest = refs[:count], refs[count : 2 * count], refs[2 * count :]
    out_ref, acc_ref = rest[-2], rest[-1]
    k = k_ref[0]
    new = count - 1
    starts = [0]
    for ref in own:
        starts.append(starts[-1] + ref.shape[0])
    out_ref[:, starts[new] :] = jnp.zeros((8, own[new].shape[0]), f32)
    if new:
        out_ref[:, 0 : starts[new]] = rest[0][...]
    acc_ref[...] = jnp.zeros_like(acc_ref)
    for row, texts in ((1, own), (2, other)):
        for j in range(count):
            keys = texts[j][:, DE:]
            col = jnp.zeros((8, keys.shape[0]), f32)
            for i in range(count) if j == new else [new]:
                for b in range(0, own[i].shape[0], TI):
                    s = lax.dot_general(own[i][b : b + TI, 0:DE], keys, NT, preferred_element_type=f32)
                    grown = jnp.exp2(s * k)
                    at = starts[i] + b
                    acc_ref[at : at + TI, :] += fold_lanes(grown)
                    col = col + fold_rows(grown)
            out_ref[row : row + 1, starts[j] : starts[j + 1]] += jnp.sum(col, axis=0, keepdims=True)
    for b in range(0, starts[-1], TI):
        out_ref[0:1, b : b + TI] += jnp.sum(acc_ref[b : b + TI, :].T, axis=0, keepdims=True)


def block_sums(k, own, other, before):
    known = sum(a.shape[0] for a in own)
    inputs = list(own) + list(other) + ([] if before is None else [before])
    flops = 4 * DE * (known * known - (0 if before is None else before.shape[1] ** 2))
    return pl.pallas_call(
        functools.partial(sums_kernel, len(own)),
        out_shape=jax.ShapeDtypeStruct((8, known), f32),
        in_specs=[SMEM_SPEC] + [VMEM_SPEC] * len(inputs),
        out_specs=VMEM_SPEC,
        scratch_shapes=[pltpu.VMEM((known, 128), f32)],
        cost_estimate=pl.CostEstimate(flops=flops, bytes_accessed=4096 * known, transcendentals=flops // (2 * DE)),
        compiler_params=PARAMS,
        name="sums",
    )(k, *inputs)


STEP = 512


def pull_kernel(count, sc_ref, sums_ref, other_ref, h_ref, e_ref, st_ref, *refs):
    arrays = refs[: 2 * count]
    q_ref, out_ref, inv_ref, grown_ref = refs[2 * count :]
    temper, bound, k = sc_ref[0], sc_ref[1], sc_ref[2]
    inv_ref[0:1, 0:HALF] = 1.0 / sums_ref[0:1, :]
    inv_ref[0:1, HALF:] = 1.0 / other_ref[0:1, :]
    inv_ref[1:2, 0:HALF] = 1.0 / (sums_ref[1:2, :] + other_ref[2:3, :])
    inv_ref[1:2, HALF:] = 1.0 / (sums_ref[2:3, :] + other_ref[1:2, :])
    parts, at = [], 0
    for ref in arrays:
        for b in range(0, ref.shape[0], STEP):
            size = min(STEP, ref.shape[0] - b)
            parts.append((ref, slice(b, b + size), slice(at, at + size)))
            at += size
    loss = jnp.zeros((BD, 1), f32)
    square = jnp.full((BD, 1), 1e-06, f32)
    grads = []
    for side in range(2):
        away = 1 - side
        half = slice(DE * away, DE * (away + 1))
        own = h_ref[:, DE * side : DE * (side + 1)]
        total = jnp.zeros((BD, 128), f32)
        for ref, rows, place_ in parts:
            s = lax.dot_general(own, ref[rows, half], NT, preferred_element_type=f32)
            grown = jnp.exp2(s * k)
            grown_ref[:, place_] = grown
            total = total + fold_lanes(grown)
        total = jnp.sum(total, axis=1, keepdims=True)
        own_inv = 1.0 / total
        d = jnp.zeros((BD, DE), f32)
        for ref, rows, place_ in parts:
            w = (grown_ref[:, place_] * (own_inv + inv_ref[away : away + 1, place_])).astype(bf16)
            d = d + jnp.dot(w, ref[rows, half], preferred_element_type=f32)
        f_own = own.astype(f32)
        f_away = h_ref[:, half].astype(f32)
        diag = temper * jnp.sum(f_own * f_away, axis=1, keepdims=True)
        loss = loss + (jnp.log(total) - diag)
        d = temper * d - 2.0 * temper * f_away
        e = e_ref[:, DE * side : DE * (side + 1)]
        inv = st_ref[:, 256 * side : 256 * side + 1]
        size = st_ref[:, 256 * side + 128 : 256 * side + 129]
        grad = (d - e * jnp.sum(e * d, axis=1, keepdims=True)) * inv
        square = square + size * jnp.sum(grad * grad, axis=1, keepdims=True)
        grads.append(grad)
    norm = jnp.sqrt(square)
    factor = jnp.minimum(1.0, bound / norm)
    count_ = 1.0 / (1.0 + jnp.exp((norm - bound) / (0.1 * bound)))
    for side in range(2):
        q = (factor * grads[side]).T.astype(bf16)
        q_ref[:, PER_YC * side : PER_YC * (side + 1), :] = q.reshape(NYC, PER_YC, BD)
    out_ref[0:1, :] = jnp.broadcast_to(jnp.sum(loss, axis=0, keepdims=True), (1, 128))
    out_ref[1:2, :] = jnp.broadcast_to(jnp.sum(count_, axis=0, keepdims=True), (1, 128))
    out_ref[2:8, :] = jnp.zeros((6, 128), f32)


def pull(scalars, sums, theirs, h, e, stats, own, other):
    return pl.pallas_call(
        functools.partial(pull_kernel, len(own)),
        out_shape=(
            jax.ShapeDtypeStruct((NYC, 2 * PER_YC, BD), bf16),
            jax.ShapeDtypeStruct((8, 128), f32),
        ),
        in_specs=[SMEM_SPEC] + [VMEM_SPEC] * (5 + 2 * len(own)),
        out_specs=[VMEM_SPEC] * 2,
        scratch_shapes=[pltpu.VMEM((8, ROWS), f32), pltpu.VMEM((BD, ROWS), f32)],
        compiler_params=PARAMS,
        name="pull",
    )(scalars, sums, theirs, h, e, stats, *own, *other)


FROM = (0, 1, 3, 2)


def share_kernel(core_ref, q_ref, f_ref, g_ref, part_ref, out_ref):
    core, y = core_ref[0], core_ref[1]
    lane = lax.broadcasted_iota(jnp.int32, (PER_X, 128), 1)
    tail = jnp.where(lane < 3, part_ref[0:1, :], jnp.where(lane < 6, part_ref[1:2, :], 0.0))
    for side, (low, width) in enumerate(((0, DI), (DI, DT))):
        rows = slice(PER_YC * side, PER_YC * (side + 1))
        total = jnp.zeros((PER_YC, width), f32)
        for ref, which in ((f_ref, core), (g_ref, 1 - core)):
            places = [lax.rem(y + NY - back, NY) for back in FROM]
            left = jnp.concatenate([q_ref[NC * at + which, rows, :] for at in places], axis=1)
            right = ref[:, low : low + width]
            total = total + jnp.dot(left, right, preferred_element_type=f32)
        for x in range(NX):
            out_ref[x, :, low : low + width] = total[PER_X * x : PER_X * (x + 1), :]
    for x in range(NX):
        out_ref[x, :, WIDE:] = tail


def share(core, q, feats, others, part):
    return pl.pallas_call(
        share_kernel,
        out_shape=jax.ShapeDtypeStruct((NX, PER_X, LONG), f32),
        in_specs=[SMEM_SPEC] + [VMEM_SPEC] * 4,
        out_specs=VMEM_SPEC,
        compiler_params=PARAMS,
        name="share",
    )(core, q, feats, others, part)


def finish_kernel(sc_ref, v_ref, noise_ref, out_ref):
    bound = sc_ref[1]
    total = v_ref[0]
    for k in range(1, NZ):
        total = total + v_ref[k]
    grad = (total + bound * noise_ref[...]) / bound
    rest = total[:, WIDE:]
    lane = lax.broadcasted_iota(jnp.int32, (1, 128), 1)
    packed = jnp.zeros((1, 128), f32)
    for n in range(3):
        term = rest.astype(bf16).astype(f32)
        packed = jnp.where((lane == n) | (lane == 3 + n), term, packed)
        rest = rest - term
    rows = [grad[:, 128 * k : 128 * (k + 1)] for k in range(WIDE // 128)] + [packed]
    out = jnp.concatenate(rows + [jnp.zeros((16 - len(rows), 128), f32)], axis=0).astype(bf16)
    for k in range(NZ):
        out_ref[k] = out


def finish(scalars, received, noise):
    return pl.pallas_call(
        finish_kernel,
        out_shape=jax.ShapeDtypeStruct((NZ, 16, 128), bf16),
        in_specs=[SMEM_SPEC] + [VMEM_SPEC] * 2,
        out_specs=VMEM_SPEC,
        compiler_params=PARAMS,
        name="finish",
    )(scalars, received, noise)


def final_kernel(core_ref, a_ref, b_ref, gi_ref, gt_ref, sum_ref):
    core = core_ref[0]
    mine, theirs = a_ref[...], b_ref[...]
    both = (jnp.where(core == 0, mine, theirs), jnp.where(core == 0, theirs, mine))
    for k in range(WIDE // 128):
        part = slice(128 * k, 128 * (k + 1))
        rows = [both[c][NY * x + y, :, part] for y in range(NY) for c in range(NC) for x in range(NX)]
        block = jnp.concatenate(rows, axis=0).T
        if k < DI // 128:
            gi_ref[part, :] = block
        else:
            gt_ref[128 * k - DI : 128 * (k + 1) - DI, :] = block
    tail = jnp.zeros((NZ, 128), f32)
    for y in range(NY):
        tail = tail + (both[0][y, :, WIDE:].astype(f32) + both[1][y, :, WIDE:].astype(f32))
    sum_ref[...] = tail[0:8, :]


def final(core, mine, theirs):
    return pl.pallas_call(
        final_kernel,
        out_shape=(
            jax.ShapeDtypeStruct((DI, DE), bf16),
            jax.ShapeDtypeStruct((DT, DE), bf16),
            jax.ShapeDtypeStruct((8, 128), f32),
        ),
        in_specs=[SMEM_SPEC] + [VMEM_SPEC] * 2,
        out_specs=[VMEM_SPEC] * 3,
        compiler_params=PARAMS,
        name="final",
    )(core, mine, theirs)


def place(z, xh, xl, y, c):
    return (((z * 2 + xh) * 2 + xl) * 4 + y) * 2 + c


def pairs(target):
    out = []
    for z in range(16):
        for xh in range(2):
            for xl in range(2):
                for y in range(4):
                    for c in range(2):
                        out.append((place(z, xh, xl, y, c), place(*target(z, xh, xl, y, c))))
    return out


REGROUP = pairs(lambda z, xh, xl, y, c: (z, c, xl, y, xh))
CORES = pairs(lambda z, xh, xl, y, c: (z, xh, xl, y, 1 - c))
UP = pairs(lambda z, xh, xl, y, c: ((z + 1) % NZ, xh, xl, y, c))
DOWN = pairs(lambda z, xh, xl, y, c: ((z - 1) % NZ, xh, xl, y, c))


def along_y(steps):
    return pairs(lambda z, xh, xl, y, c: (z, xh, xl, (y + steps) % NY, c))


def send(array, target):
    return lax.ppermute(array, AX, target)


def after(array, *others):
    return lax.optimization_barrier((array,) + others)[0]


def noise_column(noise, column):
    part = lax.dynamic_slice(noise, (0, column), (noise.shape[0], 1))
    return part.astype(f32).reshape(1, noise.shape[0])


def local(img_feat, txt_feat, img_proj, txt_proj, logit_scale, clip_bound, noise_img, noise_txt, noise_count):
    temper, bound = logit_scale[0], clip_bound[0]
    z, c = lax.axis_index("z"), lax.axis_index("c")
    x, yc = lax.axis_index(XX), lax.axis_index(YC)
    core = jnp.stack([c, lax.axis_index("y")]).astype(jnp.int32)
    k = logit_scale * math.log2(math.e)
    scalars = jnp.concatenate([logit_scale, clip_bound, k])
    feats = send(jnp.concatenate([img_feat, txt_feat], axis=1), REGROUP)
    h, e, stats = embed(feats, img_proj, txt_proj)
    column = PER_YC * yc + PER_X * x + z
    noise = jnp.concatenate(
        [noise_column(noise_img, column), noise_column(noise_txt, column), jnp.zeros((1, 128), f32)], axis=1
    )
    up, down = [h], [h]
    own, other = [], []
    near = [feats]

    def lot(blocks):
        own.append(jnp.concatenate(blocks, axis=0))
        other.append(send(own[-1], CORES))

    def step(*waits):
        ups, downs = up[-1], down[-1]
        if waits:
            ups, downs = lax.optimization_barrier((ups, downs) + waits)[0:2]
        up.append(send(ups, UP))
        if len(up) <= NZ // 2:
            down.append(send(downs, DOWN))

    step()
    near.append(send(after(feats, h), along_y(1)))
    step()
    near.append(send(after(feats, up[1]), along_y(3)))
    step(near[1])
    near.append(send(after(feats, up[2]), along_y(2)))
    step(near[2], noise)
    step()
    lot([up[1], down[1], up[2], down[2], up[3], down[3], up[4], down[4]])
    near = jnp.concatenate(near, axis=0)
    step(near, other[0])
    beside = send(near, CORES)
    sums = block_sums(k, own, other, None)
    lot([up[5], down[5], up[6], down[6]])
    step()
    lot([up[7], down[7]])
    step(other[1], beside, sums)
    sums = block_sums(k, own[0:2], other[0:2], sums)
    lot([after(h, sums), up[8]])
    sums = block_sums(k, own[0:3], other[0:3], sums)
    sums = block_sums(k, own, other, sums)
    q, part = pull(scalars, sums, send(sums, CORES), h, e, stats, own, other)
    q = lax.all_to_all(q, YC, 0, 0)
    mine = lax.all_to_all(share(core, q, near, beside, part), XX, 0, 0)
    mine = jnp.sum(mine, axis=0).reshape(NZ, 1, LONG)
    mine = finish(scalars, lax.all_to_all(mine, "z", 0, 0), noise)
    mine = lax.all_to_all(mine, "z", 0, 0)[:, 0 : LONG // 128, :].reshape(NZ, LONG)
    mine = lax.all_to_all(jnp.broadcast_to(mine[None], (NXY, NZ, LONG)), XY, 0, 0)
    theirs = lax.ppermute(mine, AX, CORES)
    grad_img, grad_txt, tail = final(core, mine, theirs)
    loss = (tail[0, 0] + tail[0, 1] + tail[0, 2]) / (2.0 * BATCH)
    count = tail[0, 3] + tail[0, 4] + tail[0, 5]
    frac = (count + 0.05 * BATCH * noise_count[0]) / BATCH
    new_bound = bound * jnp.exp(-0.2 * (frac - 0.5))
    return grad_img, grad_txt, jnp.reshape(loss, (1,)), jnp.reshape(new_bound, (1,))


def solution(mesh):
    fine = Mesh(mesh.devices.reshape(DIMS), AX)
    whole = P()
    return jax.shard_map(
        local,
        mesh=fine,
        in_specs=(P(AX, None), P(AX, None)) + (whole,) * 7,
        out_specs=(whole,) * 4,
        check_vma=False,
    )
```

```python
import functools
import math

import jax
import jax.numpy as jnp
from jax import lax
from jax.experimental import pallas as pl
from jax.experimental.pallas import tpu as pltpu
from jax.sharding import Mesh, PartitionSpec as P

AX = ("z", "xh", "xl", "y", "c")
XY = ("xh", "xl", "y")
PLANE = ("xh", "xl", "y", "c")
DIMS = (16, 2, 2, 4, 2)
DI, DT, DE, BD = 768, 512, 512, 128
WIDE = DI + DT
ROWS = 4096
HALF = ROWS // 2
NXY, NC, NZ = 16, 2, 16
NPL = NXY * NC
PER = DE // NPL
BATCH = 65536
LONG = WIDE + 128
bf16, f32 = jnp.bfloat16, jnp.float32
NT = (((1,), (1,)), ((), ()))
VMEM_SPEC = pl.BlockSpec(memory_space=pltpu.VMEM)
SMEM_SPEC = pl.BlockSpec(memory_space=pltpu.SMEM)
PARAMS = pltpu.CompilerParams(vmem_limit_bytes=32 * 1024 * 1024)


def fold_lanes(x):
    total = x[:, 0:128]
    for k in range(1, x.shape[1] // 128):
        total = total + x[:, 128 * k : 128 * (k + 1)]
    return total


def fold_rows(x):
    total = x[0:8, :]
    for k in range(1, x.shape[0] // 8):
        total = total + x[8 * k : 8 * (k + 1), :]
    return total


def embed_kernel(f_ref, pi_ref, pt_ref, h_ref, e_ref, st_ref):
    for side, (low, width, p_ref) in enumerate(((0, DI, pi_ref), (DI, DT, pt_ref))):
        x = f_ref[:, low : low + width]
        u = jnp.dot(x, p_ref[...], preferred_element_type=f32)
        inv = lax.rsqrt(jnp.sum(u * u, axis=1, keepdims=True) + 1e-06)
        e = u * inv
        e_ref[:, DE * side : DE * (side + 1)] = e
        h_ref[:, DE * side : DE * (side + 1)] = e.astype(bf16)
        xf = x.astype(f32)
        size = jnp.sum(xf * xf, axis=1, keepdims=True)
        st_ref[:, 256 * side : 256 * side + 128] = jnp.broadcast_to(inv, (BD, 128))
        st_ref[:, 256 * side + 128 : 256 * side + 256] = jnp.broadcast_to(size, (BD, 128))


def embed(feats, img_proj, txt_proj):
    return pl.pallas_call(
        embed_kernel,
        out_shape=(
            jax.ShapeDtypeStruct((BD, 2 * DE), bf16),
            jax.ShapeDtypeStruct((BD, 2 * DE), f32),
            jax.ShapeDtypeStruct((BD, 512), f32),
        ),
        in_specs=[VMEM_SPEC] * 3,
        out_specs=[VMEM_SPEC] * 3,
        compiler_params=PARAMS,
        name="embed",
    )(feats, img_proj, txt_proj)


TI, TJ = 256, 1024


def lse_kernel(core_ref, k_ref, g_ref, col_ref, row_ref, acc_ref):
    k = k_ref[0]
    first = pl.multiple_of(core_ref[0] * HALF, HALF)
    acc_ref[...] = jnp.zeros_like(acc_ref)
    for j in range(ROWS // TJ):
        keys = g_ref[j * TJ : (j + 1) * TJ, DE:]
        col = jnp.zeros((8, TJ), f32)
        for b in range(HALF // TI):
            rows = g_ref[pl.ds(pl.multiple_of(first + b * TI, TI), TI), 0:DE]
            s = lax.dot_general(rows, keys, NT, preferred_element_type=f32)
            grown = jnp.exp2(s * k)
            acc_ref[b * TI : (b + 1) * TI, :] += fold_lanes(grown)
            col = col + fold_rows(grown)
        col_ref[:, j * TJ : (j + 1) * TJ] = jnp.sum(col, axis=0, keepdims=True)
    for b in range(HALF // TI):
        part = acc_ref[b * TI : (b + 1) * TI, :]
        row_ref[:, b * TI : (b + 1) * TI] = jnp.sum(part.T, axis=0, keepdims=True)


def lse_sums(core, k, gathered):
    return pl.pallas_call(
        lse_kernel,
        out_shape=(
            jax.ShapeDtypeStruct((1, ROWS), f32),
            jax.ShapeDtypeStruct((1, HALF), f32),
        ),
        in_specs=[SMEM_SPEC] * 2 + [VMEM_SPEC],
        out_specs=[VMEM_SPEC] * 2,
        scratch_shapes=[pltpu.VMEM((HALF, 128), f32)],
        compiler_params=PARAMS,
        name="lse",
    )(core, k, gathered)


STEP = 512


def pull_kernel(core_ref, sc_ref, sums_ref, other_ref, g_ref, h_ref, e_ref, st_ref, q_ref, out_ref, inv_ref, grown_ref):
    core = core_ref[0]
    temper, bound, k = sc_ref[0], sc_ref[1], sc_ref[2]
    inv_ref[1:2, :] = 1.0 / (sums_ref[:, 0:ROWS] + other_ref[:, 0:ROWS])
    mine, theirs = 1.0 / sums_ref[:, ROWS:], 1.0 / other_ref[:, ROWS:]
    inv_ref[0:1, 0:HALF] = jnp.where(core == 0, mine, theirs)
    inv_ref[0:1, HALF:] = jnp.where(core == 0, theirs, mine)
    loss = jnp.zeros((BD, 1), f32)
    square = jnp.full((BD, 1), 1e-06, f32)
    grads = []
    step = STEP
    for side in range(2):
        away = 1 - side
        own = h_ref[:, DE * side : DE * (side + 1)]
        total = jnp.zeros((BD, 128), f32)
        for j in range(ROWS // step):
            keys = g_ref[j * step : (j + 1) * step, DE * away : DE * (away + 1)]
            s = lax.dot_general(own, keys, NT, preferred_element_type=f32)
            grown = jnp.exp2(s * k)
            grown_ref[:, j * step : (j + 1) * step] = grown
            total = total + fold_lanes(grown)
        total = jnp.sum(total, axis=1, keepdims=True)
        own_inv = 1.0 / total
        d = jnp.zeros((BD, DE), f32)
        for j in range(ROWS // step):
            keys = g_ref[j * step : (j + 1) * step, DE * away : DE * (away + 1)]
            far = inv_ref[away : away + 1, j * step : (j + 1) * step]
            w = (grown_ref[:, j * step : (j + 1) * step] * (own_inv + far)).astype(bf16)
            d = d + jnp.dot(w, keys, preferred_element_type=f32)
        f_own = own.astype(f32)
        f_away = h_ref[:, DE * away : DE * (away + 1)].astype(f32)
        diag = temper * jnp.sum(f_own * f_away, axis=1, keepdims=True)
        loss = loss + (jnp.log(total) - diag)
        d = temper * d - 2.0 * temper * f_away
        e = e_ref[:, DE * side : DE * (side + 1)]
        inv = st_ref[:, 256 * side : 256 * side + 1]
        size = st_ref[:, 256 * side + 128 : 256 * side + 129]
        grad = (d - e * jnp.sum(e * d, axis=1, keepdims=True)) * inv
        square = square + size * jnp.sum(grad * grad, axis=1, keepdims=True)
        grads.append(grad)
    norm = jnp.sqrt(square)
    factor = jnp.minimum(1.0, bound / norm)
    count = 1.0 / (1.0 + jnp.exp((norm - bound) / (0.1 * bound)))
    for side in range(2):
        q = (factor * grads[side]).T.astype(bf16)
        q_ref[:, PER * side : PER * (side + 1), :] = q.reshape(NPL, PER, BD)
    out_ref[0:1, :] = jnp.broadcast_to(jnp.sum(loss, axis=0, keepdims=True), (1, 128))
    out_ref[1:2, :] = jnp.broadcast_to(jnp.sum(count, axis=0, keepdims=True), (1, 128))
    out_ref[2:8, :] = jnp.zeros((6, 128), f32)


def pull(core, scalars, sums, other, gathered, h, e, stats):
    return pl.pallas_call(
        pull_kernel,
        out_shape=(
            jax.ShapeDtypeStruct((NPL, 2 * PER, BD), bf16),
            jax.ShapeDtypeStruct((8, 128), f32),
        ),
        in_specs=[SMEM_SPEC] * 2 + [VMEM_SPEC] * 6,
        out_specs=[VMEM_SPEC] * 2,
        scratch_shapes=[
            pltpu.VMEM((2, ROWS), f32),
            pltpu.VMEM((BD, ROWS), f32),
        ],
        compiler_params=PARAMS,
        name="pull",
    )(core, scalars, sums, other, gathered, h, e, stats)


def share_kernel(core_ref, q_ref, f_ref, g_ref, part_ref, out_ref):
    core = core_ref[0]
    lane = lax.broadcasted_iota(jnp.int32, (1, 128), 1)
    tail = jnp.where(lane < 3, part_ref[0:1, :], jnp.where(lane < 6, part_ref[1:2, :], 0.0))
    sums = []
    for side, (low, width) in enumerate(((0, DI), (DI, DT))):
        rows = slice(PER * side, PER * (side + 1))
        total = jnp.zeros((PER, width), f32)
        for ref, which in ((f_ref, core), (g_ref, 1 - core)):
            left = jnp.concatenate([q_ref[NC * p + which, rows, :] for p in range(NXY)], axis=1)
            right = ref[:, :, low : low + width].reshape(NXY * BD, width)
            total = total + jnp.dot(left, right, preferred_element_type=f32)
        sums.append(total)
    for m in range(PER):
        out_ref[m, :, 0:DI] = sums[0][m : m + 1, :]
        out_ref[m, :, DI:WIDE] = sums[1][m : m + 1, :]
        out_ref[m, :, WIDE:] = tail


def share(core, q, feats, others, part):
    return pl.pallas_call(
        share_kernel,
        out_shape=jax.ShapeDtypeStruct((PER, 1, LONG), f32),
        in_specs=[SMEM_SPEC] + [VMEM_SPEC] * 4,
        out_specs=VMEM_SPEC,
        compiler_params=PARAMS,
        name="share",
    )(core, q, feats, others, part)


def finish_kernel(sc_ref, v_ref, noise_ref, out_ref):
    bound = sc_ref[1]
    total = v_ref[0]
    for k in range(1, NZ):
        total = total + v_ref[k]
    grad = (total + bound * noise_ref[...]) / bound
    rest = total[:, WIDE:]
    lane = lax.broadcasted_iota(jnp.int32, (1, 128), 1)
    packed = jnp.zeros((1, 128), f32)
    for n in range(3):
        term = rest.astype(bf16).astype(f32)
        packed = jnp.where((lane == n) | (lane == 3 + n), term, packed)
        rest = rest - term
    rows = [grad[:, 128 * k : 128 * (k + 1)] for k in range(WIDE // 128)] + [packed]
    out = jnp.concatenate(rows + [jnp.zeros((16 - len(rows), 128), f32)], axis=0).astype(bf16)
    for k in range(NZ):
        out_ref[k] = out


def finish(scalars, received, noise):
    return pl.pallas_call(
        finish_kernel,
        out_shape=jax.ShapeDtypeStruct((NZ, 16, 128), bf16),
        in_specs=[SMEM_SPEC] + [VMEM_SPEC] * 2,
        out_specs=VMEM_SPEC,
        compiler_params=PARAMS,
        name="finish",
    )(scalars, received, noise)


def final_kernel(core_ref, a_ref, b_ref, gi_ref, gt_ref, sum_ref):
    core = core_ref[0]
    mine, theirs = a_ref[...], b_ref[...]
    both = (jnp.where(core == 0, mine, theirs), jnp.where(core == 0, theirs, mine))
    for k in range(WIDE // 128):
        part = slice(128 * k, 128 * (k + 1))
        rows = [both[c][p, :, part] for p in range(NXY) for c in range(NC)]
        block = jnp.concatenate(rows, axis=0).T
        if k < DI // 128:
            gi_ref[part, :] = block
        else:
            gt_ref[128 * k - DI : 128 * (k + 1) - DI, :] = block
    tail = jnp.zeros((NZ, 128), f32)
    for p in range(NXY):
        tail = tail + (both[0][p, :, WIDE:].astype(f32) + both[1][p, :, WIDE:].astype(f32))
    sum_ref[...] = tail[0:8, :]


def final(core, mine, theirs):
    return pl.pallas_call(
        final_kernel,
        out_shape=(
            jax.ShapeDtypeStruct((DI, DE), bf16),
            jax.ShapeDtypeStruct((DT, DE), bf16),
            jax.ShapeDtypeStruct((8, 128), f32),
        ),
        in_specs=[SMEM_SPEC] + [VMEM_SPEC] * 2,
        out_specs=[VMEM_SPEC] * 3,
        compiler_params=PARAMS,
        name="final",
    )(core, mine, theirs)


def place(z, xh, xl, y, c):
    return (((z * 2 + xh) * 2 + xl) * 4 + y) * 2 + c


def pairs(target):
    out = []
    for z in range(16):
        for xh in range(2):
            for xl in range(2):
                for y in range(4):
                    for c in range(2):
                        out.append((place(z, xh, xl, y, c), place(*target(z, xh, xl, y, c))))
    return out


REGROUP = pairs(lambda z, xh, xl, y, c: (z, c, xl, y, xh))
CORES = pairs(lambda z, xh, xl, y, c: (z, xh, xl, y, 1 - c))


def noise_column(noise, column):
    part = lax.dynamic_slice(noise, (0, column), (noise.shape[0], 1))
    return part.astype(f32).reshape(1, noise.shape[0])


def local(img_feat, txt_feat, img_proj, txt_proj, logit_scale, clip_bound, noise_img, noise_txt, noise_count):
    temper, bound = logit_scale[0], clip_bound[0]
    z, c = lax.axis_index("z"), lax.axis_index("c")
    at = lax.axis_index(XY)
    core = c.astype(jnp.int32).reshape(1)
    k = logit_scale * math.log2(math.e)
    scalars = jnp.concatenate([logit_scale, clip_bound, k])
    feats = lax.ppermute(jnp.concatenate([img_feat, txt_feat], axis=1), AX, REGROUP)
    h, e, stats = embed(feats, img_proj, txt_proj)
    gathered = lax.all_gather(h, ("z", "c"), axis=0, tiled=True)
    spread = lax.all_to_all(jnp.broadcast_to(feats[None], (NXY, BD, WIDE)), XY, 0, 0)
    beside = lax.ppermute(spread, AX, CORES)
    column = PER * (NC * at + c) + z
    noise = jnp.concatenate(
        [noise_column(noise_img, column), noise_column(noise_txt, column), jnp.zeros((1, 128), f32)], axis=1
    )
    gathered, spread, noise = lax.optimization_barrier((gathered, spread, noise))
    sums = jnp.concatenate(lse_sums(core, k, gathered), axis=1)
    other = lax.ppermute(sums, AX, CORES)
    q, part = pull(core, scalars, sums, other, gathered, h, e, stats)
    q = lax.all_to_all(q, PLANE, 0, 0)
    mine = share(core, q, spread, beside, part)
    mine = finish(scalars, lax.all_to_all(mine, "z", 0, 0), noise)
    mine = lax.all_to_all(mine, "z", 0, 0)[:, 0 : LONG // 128, :].reshape(NZ, LONG)
    mine = lax.all_to_all(jnp.broadcast_to(mine[None], (NXY, NZ, LONG)), XY, 0, 0)
    theirs = lax.ppermute(mine, AX, CORES)
    grad_img, grad_txt, tail = final(core, mine, theirs)
    loss = (tail[0, 0] + tail[0, 1] + tail[0, 2]) / (2.0 * BATCH)
    count = tail[0, 3] + tail[0, 4] + tail[0, 5]
    frac = (count + 0.05 * BATCH * noise_count[0]) / BATCH
    new_bound = bound * jnp.exp(-0.2 * (frac - 0.5))
    return grad_img, grad_txt, jnp.reshape(loss, (1,)), jnp.reshape(new_bound, (1,))


def solution(mesh):
    fine = Mesh(mesh.devices.reshape(DIMS), AX)
    whole = P()
    return jax.shard_map(
        local,
        mesh=fine,
        in_specs=(P(AX, None), P(AX, None)) + (whole,) * 7,
        out_specs=(whole,) * 4,
        check_vma=False,
    )
```

```python
import functools
import math

import jax
import jax.numpy as jnp
from jax import lax
from jax.experimental import pallas as pl
from jax.experimental.pallas import tpu as pltpu
from jax.sharding import Mesh, PartitionSpec as P

AX = ("z", "xh", "xl", "y", "c")
XY = ("xh", "xl", "y")
PLANE = ("xh", "xl", "y", "c")
DIMS = (16, 2, 2, 4, 2)
DI, DT, DE, BD = 768, 512, 512, 128
WIDE = DI + DT
ROWS = 4096
HALF = ROWS // 2
NXY, NC, NZ = 16, 2, 16
NPL = NXY * NC
PER = DE // NPL
BATCH = 65536
LONG = WIDE + 128
LOG2E = math.log2(math.e)
bf16, f32 = jnp.bfloat16, jnp.float32
NT = (((1,), (1,)), ((), ()))
VMEM_SPEC = pl.BlockSpec(memory_space=pltpu.VMEM)
SMEM_SPEC = pl.BlockSpec(memory_space=pltpu.SMEM)
PARAMS = pltpu.CompilerParams(vmem_limit_bytes=16 * 1024 * 1024)


def fold_lanes(x):
    total = x[:, 0:128]
    for k in range(1, x.shape[1] // 128):
        total = total + x[:, 128 * k : 128 * (k + 1)]
    return total


def fold_rows(x):
    total = x[0:8, :]
    for k in range(1, x.shape[0] // 8):
        total = total + x[8 * k : 8 * (k + 1), :]
    return total


def embed_kernel(f_ref, pi_ref, pt_ref, h_ref, e_ref, st_ref):
    for side, (low, width, p_ref) in enumerate(((0, DI, pi_ref), (DI, DT, pt_ref))):
        x = f_ref[:, low : low + width]
        u = jnp.dot(x, p_ref[...], preferred_element_type=f32)
        inv = lax.rsqrt(jnp.sum(u * u, axis=1, keepdims=True) + 1e-06)
        e = u * inv
        e_ref[:, DE * side : DE * (side + 1)] = e
        h_ref[:, DE * side : DE * (side + 1)] = e.astype(bf16)
        xf = x.astype(f32)
        size = jnp.sum(xf * xf, axis=1, keepdims=True)
        st_ref[:, 256 * side : 256 * side + 128] = jnp.broadcast_to(inv, (BD, 128))
        st_ref[:, 256 * side + 128 : 256 * side + 256] = jnp.broadcast_to(size, (BD, 128))


def embed(feats, img_proj, txt_proj):
    return pl.pallas_call(
        embed_kernel,
        out_shape=(
            jax.ShapeDtypeStruct((BD, 2 * DE), bf16),
            jax.ShapeDtypeStruct((BD, 2 * DE), f32),
            jax.ShapeDtypeStruct((BD, 512), f32),
        ),
        in_specs=[VMEM_SPEC] * 3,
        out_specs=[VMEM_SPEC] * 3,
        compiler_params=PARAMS,
        name="embed",
    )(feats, img_proj, txt_proj)


TI, TJ = 256, 1024


def lse_kernel(core_ref, scale_ref, g_ref, col_ref, row_ref, acc_ref):
    k = scale_ref[0] * LOG2E
    first = pl.multiple_of(core_ref[0] * HALF, HALF)
    acc_ref[...] = jnp.zeros_like(acc_ref)
    for j in range(ROWS // TJ):
        keys = g_ref[j * TJ : (j + 1) * TJ, DE:]
        col = jnp.zeros((8, TJ), f32)
        for b in range(HALF // TI):
            rows = g_ref[pl.ds(pl.multiple_of(first + b * TI, TI), TI), 0:DE]
            s = lax.dot_general(rows, keys, NT, preferred_element_type=f32)
            grown = jnp.exp2(s * k)
            acc_ref[b * TI : (b + 1) * TI, :] += fold_lanes(grown)
            col = col + fold_rows(grown)
        col_ref[:, j * TJ : (j + 1) * TJ] = jnp.sum(col, axis=0, keepdims=True)
    for b in range(HALF // TI):
        part = acc_ref[b * TI : (b + 1) * TI, :]
        row_ref[:, b * TI : (b + 1) * TI] = jnp.sum(part.T, axis=0, keepdims=True)


def lse_sums(core, scale, gathered):
    return pl.pallas_call(
        lse_kernel,
        out_shape=(
            jax.ShapeDtypeStruct((1, ROWS), f32),
            jax.ShapeDtypeStruct((1, HALF), f32),
        ),
        in_specs=[SMEM_SPEC] * 2 + [VMEM_SPEC],
        out_specs=[VMEM_SPEC] * 2,
        scratch_shapes=[pltpu.VMEM((HALF, 128), f32)],
        compiler_params=PARAMS,
        name="lse",
    )(core, scale, gathered)


STEP = 512


def pull_kernel(core_ref, scale_ref, clip_ref, sums_ref, other_ref, g_ref, h_ref, e_ref, st_ref, q_ref, out_ref, inv_ref, grown_ref):
    core = core_ref[0]
    temper, bound = scale_ref[0], clip_ref[0]
    k = temper * LOG2E
    inv_ref[1:2, :] = 1.0 / (sums_ref[:, 0:ROWS] + other_ref[:, 0:ROWS])
    mine, theirs = 1.0 / sums_ref[:, ROWS:], 1.0 / other_ref[:, ROWS:]
    inv_ref[0:1, 0:HALF] = jnp.where(core == 0, mine, theirs)
    inv_ref[0:1, HALF:] = jnp.where(core == 0, theirs, mine)
    loss = jnp.zeros((BD, 1), f32)
    square = jnp.full((BD, 1), 1e-06, f32)
    grads = []
    step = STEP
    for side in range(2):
        away = 1 - side
        own = h_ref[:, DE * side : DE * (side + 1)]
        total = jnp.zeros((BD, 128), f32)
        for j in range(ROWS // step):
            keys = g_ref[j * step : (j + 1) * step, DE * away : DE * (away + 1)]
            s = lax.dot_general(own, keys, NT, preferred_element_type=f32)
            grown = jnp.exp2(s * k)
            grown_ref[:, j * step : (j + 1) * step] = grown
            total = total + fold_lanes(grown)
        total = jnp.sum(total, axis=1, keepdims=True)
        own_inv = 1.0 / total
        d = jnp.zeros((BD, DE), f32)
        for j in range(ROWS // step):
            keys = g_ref[j * step : (j + 1) * step, DE * away : DE * (away + 1)]
            far = inv_ref[away : away + 1, j * step : (j + 1) * step]
            w = (grown_ref[:, j * step : (j + 1) * step] * (own_inv + far)).astype(bf16)
            d = d + jnp.dot(w, keys, preferred_element_type=f32)
        f_own = own.astype(f32)
        f_away = h_ref[:, DE * away : DE * (away + 1)].astype(f32)
        diag = temper * jnp.sum(f_own * f_away, axis=1, keepdims=True)
        loss = loss + (jnp.log(total) - diag)
        d = temper * d - 2.0 * temper * f_away
        e = e_ref[:, DE * side : DE * (side + 1)]
        inv = st_ref[:, 256 * side : 256 * side + 1]
        size = st_ref[:, 256 * side + 128 : 256 * side + 129]
        grad = (d - e * jnp.sum(e * d, axis=1, keepdims=True)) * inv
        square = square + size * jnp.sum(grad * grad, axis=1, keepdims=True)
        grads.append(grad)
    norm = jnp.sqrt(square)
    factor = jnp.minimum(1.0, bound / norm)
    count = 1.0 / (1.0 + jnp.exp((norm - bound) / (0.1 * bound)))
    for side in range(2):
        q = (factor * grads[side]).T.astype(bf16)
        q_ref[:, PER * side : PER * (side + 1), :] = q.reshape(NPL, PER, BD)
    out_ref[0:1, :] = jnp.broadcast_to(jnp.sum(loss, axis=0, keepdims=True), (1, 128))
    out_ref[1:2, :] = jnp.broadcast_to(jnp.sum(count, axis=0, keepdims=True), (1, 128))
    out_ref[2:8, :] = jnp.zeros((6, 128), f32)


def pull(core, scale, clip_bound, sums, other, gathered, h, e, stats):
    return pl.pallas_call(
        pull_kernel,
        out_shape=(
            jax.ShapeDtypeStruct((NPL, 2 * PER, BD), bf16),
            jax.ShapeDtypeStruct((8, 128), f32),
        ),
        in_specs=[SMEM_SPEC] * 3 + [VMEM_SPEC] * 6,
        out_specs=[VMEM_SPEC] * 2,
        scratch_shapes=[
            pltpu.VMEM((2, ROWS), f32),
            pltpu.VMEM((BD, ROWS), f32),
        ],
        compiler_params=PARAMS,
        name="pull",
    )(core, scale, clip_bound, sums, other, gathered, h, e, stats)


def share_kernel(core_ref, q_ref, f_ref, g_ref, part_ref, out_ref):
    core = core_ref[0]
    lane = lax.broadcasted_iota(jnp.int32, (1, 128), 1)
    tail = jnp.where(lane < 3, part_ref[0:1, :], jnp.where(lane < 6, part_ref[1:2, :], 0.0))
    sums = []
    for side, (low, width) in enumerate(((0, DI), (DI, DT))):
        rows = slice(PER * side, PER * (side + 1))
        total = jnp.zeros((PER, width), f32)
        for ref, which in ((f_ref, core), (g_ref, 1 - core)):
            left = jnp.concatenate([q_ref[NC * p + which, rows, :] for p in range(NXY)], axis=1)
            right = ref[:, :, low : low + width].reshape(NXY * BD, width)
            total = total + jnp.dot(left, right, preferred_element_type=f32)
        sums.append(total)
    for m in range(PER):
        out_ref[m, :, 0:DI] = sums[0][m : m + 1, :]
        out_ref[m, :, DI:WIDE] = sums[1][m : m + 1, :]
        out_ref[m, :, WIDE:] = tail


def share(core, q, feats, others, part):
    return pl.pallas_call(
        share_kernel,
        out_shape=jax.ShapeDtypeStruct((PER, 1, LONG), f32),
        in_specs=[SMEM_SPEC] + [VMEM_SPEC] * 4,
        out_specs=VMEM_SPEC,
        compiler_params=PARAMS,
        name="share",
    )(core, q, feats, others, part)


def finish_kernel(clip_ref, v_ref, noise_ref, out_ref):
    bound = clip_ref[0]
    total = v_ref[0]
    for k in range(1, NZ):
        total = total + v_ref[k]
    grad = (total + bound * noise_ref[...]) / bound
    rest = total[:, WIDE:]
    lane = lax.broadcasted_iota(jnp.int32, (1, 128), 1)
    packed = jnp.zeros((1, 128), f32)
    for n in range(3):
        term = rest.astype(bf16).astype(f32)
        packed = jnp.where((lane == n) | (lane == 3 + n), term, packed)
        rest = rest - term
    rows = [grad[:, 128 * k : 128 * (k + 1)] for k in range(WIDE // 128)] + [packed]
    out = jnp.concatenate(rows + [jnp.zeros((16 - len(rows), 128), f32)], axis=0).astype(bf16)
    for k in range(NZ):
        out_ref[k] = out


def finish(clip_bound, received, noise):
    return pl.pallas_call(
        finish_kernel,
        out_shape=jax.ShapeDtypeStruct((NZ, 16, 128), bf16),
        in_specs=[SMEM_SPEC] + [VMEM_SPEC] * 2,
        out_specs=VMEM_SPEC,
        compiler_params=PARAMS,
        name="finish",
    )(clip_bound, received, noise)


def final_kernel(core_ref, clip_ref, noise_ref, a_ref, b_ref, gi_ref, gt_ref, loss_ref, bound_ref):
    core = core_ref[0]
    mine, theirs = a_ref[...], b_ref[...]
    both = (jnp.where(core == 0, mine, theirs), jnp.where(core == 0, theirs, mine))
    for k in range(WIDE // 128):
        part = slice(128 * k, 128 * (k + 1))
        rows = [both[c][p, :, part] for p in range(NXY) for c in range(NC)]
        block = jnp.concatenate(rows, axis=0).T
        if k < DI // 128:
            gi_ref[part, :] = block
        else:
            gt_ref[128 * k - DI : 128 * (k + 1) - DI, :] = block
    tail = jnp.zeros((NZ, 128), f32)
    for p in range(NXY):
        tail = tail + (both[0][p, :, WIDE:].astype(f32) + both[1][p, :, WIDE:].astype(f32))
    row = tail[0:1, :]
    lane = lax.broadcasted_iota(jnp.int32, (1, 128), 1)
    loss = jnp.sum(jnp.where(lane < 3, row, 0.0), axis=1, keepdims=True)
    count = jnp.sum(jnp.where((lane >= 3) & (lane < 6), row, 0.0), axis=1, keepdims=True)
    frac = (count + 0.05 * BATCH * noise_ref[0]) / BATCH
    bound = clip_ref[0] * jnp.exp(-0.2 * (frac - 0.5))
    loss_ref[0] = jnp.sum(loss / (2.0 * BATCH))
    bound_ref[0] = jnp.sum(bound)


def final(core, clip_bound, noise_count, mine, theirs):
    return pl.pallas_call(
        final_kernel,
        out_shape=(
            jax.ShapeDtypeStruct((DI, DE), bf16),
            jax.ShapeDtypeStruct((DT, DE), bf16),
            jax.ShapeDtypeStruct((1,), f32),
            jax.ShapeDtypeStruct((1,), f32),
        ),
        in_specs=[SMEM_SPEC] * 3 + [VMEM_SPEC] * 2,
        out_specs=[VMEM_SPEC] * 2 + [SMEM_SPEC] * 2,
        compiler_params=PARAMS,
        name="final",
    )(core, clip_bound, noise_count, mine, theirs)


def place(z, xh, xl, y, c):
    return (((z * 2 + xh) * 2 + xl) * 4 + y) * 2 + c


def pairs(target):
    out = []
    for z in range(16):
        for xh in range(2):
            for xl in range(2):
                for y in range(4):
                    for c in range(2):
                        out.append((place(z, xh, xl, y, c), place(*target(z, xh, xl, y, c))))
    return out


REGROUP = pairs(lambda z, xh, xl, y, c: (z, c, xl, y, xh))
CORES = pairs(lambda z, xh, xl, y, c: (z, xh, xl, y, 1 - c))


def noise_column(noise, column):
    part = lax.dynamic_slice(noise, (0, column), (noise.shape[0], 1))
    return part.astype(f32).reshape(1, noise.shape[0])


def local(img_feat, txt_feat, img_proj, txt_proj, logit_scale, clip_bound, noise_img, noise_txt, noise_count):
    z, c = lax.axis_index("z"), lax.axis_index("c")
    at = lax.axis_index(XY)
    core = c.astype(jnp.int32).reshape(1)
    feats = lax.ppermute(jnp.concatenate([img_feat, txt_feat], axis=1), AX, REGROUP)
    h, e, stats = embed(feats, img_proj, txt_proj)
    gathered = lax.all_gather(h, ("z", "c"), axis=0, tiled=True)
    spread = lax.all_to_all(jnp.broadcast_to(feats[None], (NXY, BD, WIDE)), XY, 0, 0)
    beside = lax.ppermute(spread, AX, CORES)
    column = PER * (NC * at + c) + z
    noise = jnp.concatenate(
        [noise_column(noise_img, column), noise_column(noise_txt, column), jnp.zeros((1, 128), f32)], axis=1
    )
    gathered, spread, noise = lax.optimization_barrier((gathered, spread, noise))
    sums = jnp.concatenate(lse_sums(core, logit_scale, gathered), axis=1)
    other = lax.ppermute(sums, AX, CORES)
    q, part = pull(core, logit_scale, clip_bound, sums, other, gathered, h, e, stats)
    q = lax.all_to_all(q, PLANE, 0, 0)
    mine = share(core, q, spread, beside, part)
    mine = finish(clip_bound, lax.all_to_all(mine, "z", 0, 0), noise)
    mine = lax.all_to_all(mine, "z", 0, 0)[:, 0 : LONG // 128, :].reshape(NZ, LONG)
    mine = lax.all_to_all(jnp.broadcast_to(mine[None], (NXY, NZ, LONG)), XY, 0, 0)
    theirs = lax.ppermute(mine, AX, CORES)
    return final(core, clip_bound, noise_count, mine, theirs)


def solution(mesh):
    fine = Mesh(mesh.devices.reshape(DIMS), AX)
    whole = P()
    return jax.shard_map(
        local,
        mesh=fine,
        in_specs=(P(AX, None), P(AX, None)) + (whole,) * 7,
        out_specs=(whole,) * 4,
        check_vma=False,
    )
```

```python
import functools
import math

import jax
import jax.numpy as jnp
from jax import lax
from jax.experimental import pallas as pl
from jax.experimental.pallas import tpu as pltpu
from jax.sharding import Mesh, PartitionSpec as P

AX = ("z", "xh", "xl", "y", "c")
XY = ("xh", "xl", "y")
PLANE = ("xh", "xl", "y", "c")
DIMS = (16, 2, 2, 4, 2)
DI, DT, DE, BD = 768, 512, 512, 128
WIDE = DI + DT
ROWS = 4096
HALF = ROWS // 2
NXY, NC, NZ = 16, 2, 16
NPL = NXY * NC
PER = DE // NPL
BATCH = 65536
LONG = WIDE + 128
LOG2E = math.log2(math.e)
bf16, f32 = jnp.bfloat16, jnp.float32
NT = (((1,), (1,)), ((), ()))
VMEM_SPEC = pl.BlockSpec(memory_space=pltpu.VMEM)
SMEM_SPEC = pl.BlockSpec(memory_space=pltpu.SMEM)
PARAMS = pltpu.CompilerParams(vmem_limit_bytes=16 * 1024 * 1024)


def fold_lanes(x):
    total = x[:, 0:128]
    for k in range(1, x.shape[1] // 128):
        total = total + x[:, 128 * k : 128 * (k + 1)]
    return total


def fold_rows(x):
    total = x[0:8, :]
    for k in range(1, x.shape[0] // 8):
        total = total + x[8 * k : 8 * (k + 1), :]
    return total


def embed_kernel(f_ref, pi_ref, pt_ref, h_ref, e_ref, st_ref):
    for side, (low, width, p_ref) in enumerate(((0, DI, pi_ref), (DI, DT, pt_ref))):
        x = f_ref[:, low : low + width]
        u = jnp.dot(x, p_ref[...], preferred_element_type=f32)
        inv = lax.rsqrt(jnp.sum(u * u, axis=1, keepdims=True) + 1e-06)
        e = u * inv
        e_ref[:, DE * side : DE * (side + 1)] = e
        h_ref[:, DE * side : DE * (side + 1)] = e.astype(bf16)
        xf = x.astype(f32)
        size = jnp.sum(xf * xf, axis=1, keepdims=True)
        st_ref[:, 256 * side : 256 * side + 128] = jnp.broadcast_to(inv, (BD, 128))
        st_ref[:, 256 * side + 128 : 256 * side + 256] = jnp.broadcast_to(size, (BD, 128))


def embed(feats, img_proj, txt_proj):
    return pl.pallas_call(
        embed_kernel,
        out_shape=(
            jax.ShapeDtypeStruct((BD, 2 * DE), bf16),
            jax.ShapeDtypeStruct((BD, 2 * DE), f32),
            jax.ShapeDtypeStruct((BD, 512), f32),
        ),
        in_specs=[VMEM_SPEC] * 3,
        out_specs=[VMEM_SPEC] * 3,
        compiler_params=PARAMS,
        name="embed",
    )(feats, img_proj, txt_proj)


TI, TJ = 256, 2048
LOT = 512


def lse_kernel(core_ref, *refs):
    scale_ref, rest = refs[0], refs[1:]
    images, (txt_ref, col_ref, row_ref, acc_ref) = rest[: HALF // LOT], rest[HALF // LOT :]
    j = pl.program_id(0)
    k = scale_ref[0] * LOG2E
    keys = txt_ref[...]

    @pl.when(j == 0)
    def _():
        acc_ref[...] = jnp.zeros_like(acc_ref)

    col = jnp.zeros((8, TJ), f32)
    for b in range(HALF // TI):
        at = b * TI % LOT
        rows = images[b * TI // LOT][at : at + TI, :]
        s = lax.dot_general(rows, keys, NT, preferred_element_type=f32)
        grown = jnp.exp2(s * k)
        acc_ref[b * TI : (b + 1) * TI, :] += fold_lanes(grown)
        col = col + fold_rows(grown)
    col_ref[...] = jnp.sum(col, axis=0, keepdims=True)

    @pl.when(j == ROWS // TJ - 1)
    def _():
        for b in range(HALF // TI):
            part = acc_ref[b * TI : (b + 1) * TI, :]
            row_ref[:, b * TI : (b + 1) * TI] = jnp.sum(part.T, axis=0, keepdims=True)


def lse_sums(core, scale, gathered):
    lots = HALF // LOT

    def image_lot(n):
        return pl.BlockSpec((LOT, DE), lambda j, core, scale: (lots * core[0] + n, 0))

    return pl.pallas_call(
        lse_kernel,
        grid_spec=pltpu.PrefetchScalarGridSpec(
            num_scalar_prefetch=2,
            grid=(ROWS // TJ,),
            in_specs=[image_lot(n) for n in range(lots)] + [pl.BlockSpec((TJ, DE), lambda j, core, scale: (j, 1))],
            out_specs=[
                pl.BlockSpec((1, TJ), lambda j, core, scale: (0, j)),
                pl.BlockSpec((1, HALF), lambda j, core, scale: (0, 0)),
            ],
            scratch_shapes=[pltpu.VMEM((HALF, 128), f32)],
        ),
        out_shape=(jax.ShapeDtypeStruct((1, ROWS), f32), jax.ShapeDtypeStruct((1, HALF), f32)),
        compiler_params=pltpu.CompilerParams(vmem_limit_bytes=48 * 1024 * 1024),
        name="lse",
    )(core, scale, *[gathered] * (lots + 1))


STEP = 512


def pull_kernel(core_ref, scale_ref, clip_ref, sums_ref, other_ref, g_ref, h_ref, e_ref, st_ref, q_ref, out_ref, inv_ref, grown_ref):
    core = core_ref[0]
    temper, bound = scale_ref[0], clip_ref[0]
    k = temper * LOG2E
    inv_ref[1:2, :] = 1.0 / (sums_ref[:, 0:ROWS] + other_ref[:, 0:ROWS])
    mine, theirs = 1.0 / sums_ref[:, ROWS:], 1.0 / other_ref[:, ROWS:]
    inv_ref[0:1, 0:HALF] = jnp.where(core == 0, mine, theirs)
    inv_ref[0:1, HALF:] = jnp.where(core == 0, theirs, mine)
    loss = jnp.zeros((BD, 1), f32)
    square = jnp.full((BD, 1), 1e-06, f32)
    grads = []
    step = STEP
    for side in range(2):
        away = 1 - side
        own = h_ref[:, DE * side : DE * (side + 1)]
        total = jnp.zeros((BD, 128), f32)
        for j in range(ROWS // step):
            keys = g_ref[j * step : (j + 1) * step, DE * away : DE * (away + 1)]
            s = lax.dot_general(own, keys, NT, preferred_element_type=f32)
            grown = jnp.exp2(s * k)
            grown_ref[:, j * step : (j + 1) * step] = grown
            total = total + fold_lanes(grown)
        total = jnp.sum(total, axis=1, keepdims=True)
        own_inv = 1.0 / total
        d = jnp.zeros((BD, DE), f32)
        for j in range(ROWS // step):
            keys = g_ref[j * step : (j + 1) * step, DE * away : DE * (away + 1)]
            far = inv_ref[away : away + 1, j * step : (j + 1) * step]
            w = (grown_ref[:, j * step : (j + 1) * step] * (own_inv + far)).astype(bf16)
            d = d + jnp.dot(w, keys, preferred_element_type=f32)
        f_own = own.astype(f32)
        f_away = h_ref[:, DE * away : DE * (away + 1)].astype(f32)
        diag = temper * jnp.sum(f_own * f_away, axis=1, keepdims=True)
        loss = loss + (jnp.log(total) - diag)
        d = temper * d - 2.0 * temper * f_away
        e = e_ref[:, DE * side : DE * (side + 1)]
        inv = st_ref[:, 256 * side : 256 * side + 1]
        size = st_ref[:, 256 * side + 128 : 256 * side + 129]
        grad = (d - e * jnp.sum(e * d, axis=1, keepdims=True)) * inv
        square = square + size * jnp.sum(grad * grad, axis=1, keepdims=True)
        grads.append(grad)
    norm = jnp.sqrt(square)
    factor = jnp.minimum(1.0, bound / norm)
    count = 1.0 / (1.0 + jnp.exp((norm - bound) / (0.1 * bound)))
    for side in range(2):
        q = (factor * grads[side]).T.astype(bf16)
        q_ref[:, PER * side : PER * (side + 1), :] = q.reshape(NPL, PER, BD)
    out_ref[0:1, :] = jnp.broadcast_to(jnp.sum(loss, axis=0, keepdims=True), (1, 128))
    out_ref[1:2, :] = jnp.broadcast_to(jnp.sum(count, axis=0, keepdims=True), (1, 128))
    out_ref[2:8, :] = jnp.zeros((6, 128), f32)


def pull(core, scale, clip_bound, sums, other, gathered, h, e, stats):
    return pl.pallas_call(
        pull_kernel,
        out_shape=(
            jax.ShapeDtypeStruct((NPL, 2 * PER, BD), bf16),
            jax.ShapeDtypeStruct((8, 128), f32),
        ),
        in_specs=[SMEM_SPEC] * 3 + [VMEM_SPEC] * 6,
        out_specs=[VMEM_SPEC] * 2,
        scratch_shapes=[
            pltpu.VMEM((2, ROWS), f32),
            pltpu.VMEM((BD, ROWS), f32),
        ],
        compiler_params=PARAMS,
        name="pull",
    )(core, scale, clip_bound, sums, other, gathered, h, e, stats)


GROUP = 4


def share_kernel(core_ref, q_ref, f_ref, g_ref, part_ref, out_ref, acc_ref):
    core, step = core_ref[0], pl.program_id(0)

    @pl.when(step == 0)
    def _():
        acc_ref[...] = jnp.zeros_like(acc_ref)

    for side, (low, width) in enumerate(((0, DI), (DI, DT))):
        rows = slice(PER * side, PER * (side + 1))
        for ref, which in ((f_ref, core), (g_ref, 1 - core)):
            left = jnp.concatenate([q_ref[NC * p + which, rows, :] for p in range(GROUP)], axis=1)
            right = ref[:, :, low : low + width].reshape(GROUP * BD, width)
            acc_ref[:, low : low + width] += jnp.dot(left, right, preferred_element_type=f32)

    @pl.when(step == NXY // GROUP - 1)
    def _():
        lane = lax.broadcasted_iota(jnp.int32, (1, 128), 1)
        tail = jnp.where(lane < 3, part_ref[0:1, :], jnp.where(lane < 6, part_ref[1:2, :], 0.0))
        for m in range(PER):
            out_ref[m, :, 0:WIDE] = acc_ref[m : m + 1, :]
            out_ref[m, :, WIDE:] = tail


def share(core, q, feats, others, part):
    return pl.pallas_call(
        share_kernel,
        grid_spec=pltpu.PrefetchScalarGridSpec(
            num_scalar_prefetch=1,
            grid=(NXY // GROUP,),
            in_specs=[
                pl.BlockSpec((NC * GROUP, 2 * PER, BD), lambda i, core: (i, 0, 0)),
                pl.BlockSpec((GROUP, BD, WIDE), lambda i, core: (i, 0, 0)),
                pl.BlockSpec((GROUP, BD, WIDE), lambda i, core: (i, 0, 0)),
                pl.BlockSpec((8, 128), lambda i, core: (0, 0)),
            ],
            out_specs=pl.BlockSpec((PER, 1, LONG), lambda i, core: (0, 0, 0)),
            scratch_shapes=[pltpu.VMEM((PER, WIDE), f32)],
        ),
        out_shape=jax.ShapeDtypeStruct((PER, 1, LONG), f32),
        compiler_params=PARAMS,
        name="share",
    )(core, q, feats, others, part)


def finish_kernel(clip_ref, v_ref, noise_ref, out_ref):
    bound = clip_ref[0]
    total = v_ref[0]
    for k in range(1, NZ):
        total = total + v_ref[k]
    grad = (total + bound * noise_ref[...]) / bound
    rest = total[:, WIDE:]
    lane = lax.broadcasted_iota(jnp.int32, (1, 128), 1)
    packed = jnp.zeros((1, 128), f32)
    for n in range(3):
        term = rest.astype(bf16).astype(f32)
        packed = jnp.where((lane == n) | (lane == 3 + n), term, packed)
        rest = rest - term
    rows = [grad[:, 128 * k : 128 * (k + 1)] for k in range(WIDE // 128)] + [packed]
    out = jnp.concatenate(rows + [jnp.zeros((16 - len(rows), 128), f32)], axis=0).astype(bf16)
    for k in range(NZ):
        out_ref[k] = out


def finish(clip_bound, received, noise):
    return pl.pallas_call(
        finish_kernel,
        out_shape=jax.ShapeDtypeStruct((NZ, 16, 128), bf16),
        in_specs=[SMEM_SPEC] + [VMEM_SPEC] * 2,
        out_specs=VMEM_SPEC,
        compiler_params=PARAMS,
        name="finish",
    )(clip_bound, received, noise)


def final_kernel(core_ref, clip_ref, noise_ref, a_ref, b_ref, gi_ref, gt_ref, loss_ref, bound_ref):
    core = core_ref[0]
    mine, theirs = a_ref[...], b_ref[...]
    both = (jnp.where(core == 0, mine, theirs), jnp.where(core == 0, theirs, mine))
    for k in range(WIDE // 128):
        part = slice(128 * k, 128 * (k + 1))
        rows = [both[c][p, :, part] for p in range(NXY) for c in range(NC)]
        block = jnp.concatenate(rows, axis=0).T
        if k < DI // 128:
            gi_ref[part, :] = block
        else:
            gt_ref[128 * k - DI : 128 * (k + 1) - DI, :] = block
    tail = jnp.zeros((NZ, 128), f32)
    for p in range(NXY):
        tail = tail + (both[0][p, :, WIDE:].astype(f32) + both[1][p, :, WIDE:].astype(f32))
    row = tail[0:1, :]
    lane = lax.broadcasted_iota(jnp.int32, (1, 128), 1)
    loss = jnp.sum(jnp.where(lane < 3, row, 0.0), axis=1, keepdims=True)
    count = jnp.sum(jnp.where((lane >= 3) & (lane < 6), row, 0.0), axis=1, keepdims=True)
    frac = (count + 0.05 * BATCH * noise_ref[0]) / BATCH
    bound = clip_ref[0] * jnp.exp(-0.2 * (frac - 0.5))
    loss_ref[0] = jnp.sum(loss / (2.0 * BATCH))
    bound_ref[0] = jnp.sum(bound)


def final(core, clip_bound, noise_count, mine, theirs):
    return pl.pallas_call(
        final_kernel,
        out_shape=(
            jax.ShapeDtypeStruct((DI, DE), bf16),
            jax.ShapeDtypeStruct((DT, DE), bf16),
            jax.ShapeDtypeStruct((1,), f32),
            jax.ShapeDtypeStruct((1,), f32),
        ),
        in_specs=[SMEM_SPEC] * 3 + [VMEM_SPEC] * 2,
        out_specs=[VMEM_SPEC] * 2 + [SMEM_SPEC] * 2,
        compiler_params=PARAMS,
        name="final",
    )(core, clip_bound, noise_count, mine, theirs)


def place(z, xh, xl, y, c):
    return (((z * 2 + xh) * 2 + xl) * 4 + y) * 2 + c


def pairs(target):
    out = []
    for z in range(16):
        for xh in range(2):
            for xl in range(2):
                for y in range(4):
                    for c in range(2):
                        out.append((place(z, xh, xl, y, c), place(*target(z, xh, xl, y, c))))
    return out


REGROUP = pairs(lambda z, xh, xl, y, c: (z, c, xl, y, xh))
CORES = pairs(lambda z, xh, xl, y, c: (z, xh, xl, y, 1 - c))


def noise_column(noise, column):
    part = lax.dynamic_slice(noise, (0, column), (noise.shape[0], 1))
    return part.astype(f32).reshape(1, noise.shape[0])


def local(img_feat, txt_feat, img_proj, txt_proj, logit_scale, clip_bound, noise_img, noise_txt, noise_count):
    z, c = lax.axis_index("z"), lax.axis_index("c")
    at = lax.axis_index(XY)
    core = c.astype(jnp.int32).reshape(1)
    feats = lax.ppermute(jnp.concatenate([img_feat, txt_feat], axis=1), AX, REGROUP)
    h, e, stats = embed(feats, img_proj, txt_proj)
    gathered = lax.all_gather(h, ("z", "c"), axis=0, tiled=True)
    spread = lax.all_to_all(jnp.broadcast_to(feats[None], (NXY, BD, WIDE)), XY, 0, 0)
    beside = lax.ppermute(spread, AX, CORES)
    column = PER * (NC * at + c) + z
    noise = jnp.concatenate(
        [noise_column(noise_img, column), noise_column(noise_txt, column), jnp.zeros((1, 128), f32)], axis=1
    )
    gathered, spread, noise = lax.optimization_barrier((gathered, spread, noise))
    sums = jnp.concatenate(lse_sums(core, logit_scale, gathered), axis=1)
    other = lax.ppermute(sums, AX, CORES)
    q, part = pull(core, logit_scale, clip_bound, sums, other, gathered, h, e, stats)
    q = lax.all_to_all(q, PLANE, 0, 0)
    mine = share(core, q, spread, beside, part)
    mine = finish(clip_bound, lax.all_to_all(mine, "z", 0, 0), noise)
    mine = lax.all_to_all(mine, "z", 0, 0)[:, 0 : LONG // 128, :].reshape(NZ, LONG)
    mine = lax.all_to_all(jnp.broadcast_to(mine[None], (NXY, NZ, LONG)), XY, 0, 0)
    theirs = lax.ppermute(mine, AX, CORES)
    return final(core, clip_bound, noise_count, mine, theirs)


def solution(mesh):
    fine = Mesh(mesh.devices.reshape(DIMS), AX)
    whole = P()
    return jax.shard_map(
        local,
        mesh=fine,
        in_specs=(P(AX, None), P(AX, None)) + (whole,) * 7,
        out_specs=(whole,) * 4,
        check_vma=False,
    )
```

```python
import functools
import math

import jax
import jax.numpy as jnp
from jax import lax
from jax.experimental import pallas as pl
from jax.experimental.pallas import tpu as pltpu
from jax.sharding import Mesh, PartitionSpec as P

AX = ("z", "xh", "xl", "y", "c")
XY = ("xh", "xl", "y")
PLANE = ("xh", "xl", "y", "c")
DIMS = (16, 2, 2, 4, 2)
DI, DT, DE, BD = 768, 512, 512, 128
WIDE = DI + DT
ROWS = 4096
HALF = ROWS // 2
NXY, NC, NZ = 16, 2, 16
NPL = NXY * NC
PER = DE // NPL
BATCH = 65536
LONG = WIDE + 128
LOG2E = math.log2(math.e)
bf16, f32 = jnp.bfloat16, jnp.float32
NT = (((1,), (1,)), ((), ()))
VMEM_SPEC = pl.BlockSpec(memory_space=pltpu.VMEM)
SMEM_SPEC = pl.BlockSpec(memory_space=pltpu.SMEM)
PARAMS = pltpu.CompilerParams(vmem_limit_bytes=16 * 1024 * 1024)


def fold_lanes(x):
    total = x[:, 0:128]
    for k in range(1, x.shape[1] // 128):
        total = total + x[:, 128 * k : 128 * (k + 1)]
    return total


def fold_rows(x):
    total = x[0:8, :]
    for k in range(1, x.shape[0] // 8):
        total = total + x[8 * k : 8 * (k + 1), :]
    return total


def embed_kernel(f_ref, pi_ref, pt_ref, h_ref, e_ref, st_ref):
    for side, (low, width, p_ref) in enumerate(((0, DI, pi_ref), (DI, DT, pt_ref))):
        x = f_ref[:, low : low + width]
        u = jnp.dot(x, p_ref[...], preferred_element_type=f32)
        inv = lax.rsqrt(jnp.sum(u * u, axis=1, keepdims=True) + 1e-06)
        e = u * inv
        e_ref[:, DE * side : DE * (side + 1)] = e
        h_ref[:, DE * side : DE * (side + 1)] = e.astype(bf16)
        xf = x.astype(f32)
        size = jnp.sum(xf * xf, axis=1, keepdims=True)
        st_ref[:, 256 * side : 256 * side + 128] = jnp.broadcast_to(inv, (BD, 128))
        st_ref[:, 256 * side + 128 : 256 * side + 256] = jnp.broadcast_to(size, (BD, 128))


def embed(feats, img_proj, txt_proj):
    return pl.pallas_call(
        embed_kernel,
        out_shape=(
            jax.ShapeDtypeStruct((BD, 2 * DE), bf16),
            jax.ShapeDtypeStruct((BD, 2 * DE), f32),
            jax.ShapeDtypeStruct((BD, 512), f32),
        ),
        in_specs=[VMEM_SPEC] * 3,
        out_specs=[VMEM_SPEC] * 3,
        compiler_params=pltpu.CompilerParams(vmem_limit_bytes=60 * 1024 * 1024),
        name="embed",
    )(feats, img_proj, txt_proj)


TI, TJ = 256, 2048
LOT = 512


def lse_kernel(core_ref, *refs):
    scale_ref, rest = refs[0], refs[1:]
    images, (txt_ref, col_ref, row_ref, acc_ref) = rest[: HALF // LOT], rest[HALF // LOT :]
    j = pl.program_id(0)
    k = scale_ref[0] * LOG2E
    keys = txt_ref[...]

    @pl.when(j == 0)
    def _():
        acc_ref[...] = jnp.zeros_like(acc_ref)

    col = jnp.zeros((8, TJ), f32)
    for b in range(HALF // TI):
        at = b * TI % LOT
        rows = images[b * TI // LOT][at : at + TI, :]
        s = lax.dot_general(rows, keys, NT, preferred_element_type=f32)
        grown = jnp.exp2(s * k)
        acc_ref[b * TI : (b + 1) * TI, :] += fold_lanes(grown)
        col = col + fold_rows(grown)
    col_ref[...] = jnp.sum(col, axis=0, keepdims=True)

    @pl.when(j == ROWS // TJ - 1)
    def _():
        for b in range(HALF // TI):
            part = acc_ref[b * TI : (b + 1) * TI, :]
            row_ref[:, b * TI : (b + 1) * TI] = jnp.sum(part.T, axis=0, keepdims=True)


def lse_sums(core, scale, gathered):
    lots = HALF // LOT

    def image_lot(n):
        return pl.BlockSpec((LOT, DE), lambda j, core, scale: (lots * core[0] + n, 0))

    return pl.pallas_call(
        lse_kernel,
        grid_spec=pltpu.PrefetchScalarGridSpec(
            num_scalar_prefetch=2,
            grid=(ROWS // TJ,),
            in_specs=[image_lot(n) for n in range(lots)] + [pl.BlockSpec((TJ, DE), lambda j, core, scale: (j, 1))],
            out_specs=[
                pl.BlockSpec((1, TJ), lambda j, core, scale: (0, j)),
                pl.BlockSpec((1, HALF), lambda j, core, scale: (0, 0)),
            ],
            scratch_shapes=[pltpu.VMEM((HALF, 128), f32)],
        ),
        out_shape=(jax.ShapeDtypeStruct((1, ROWS), f32), jax.ShapeDtypeStruct((1, HALF), f32)),
        compiler_params=pltpu.CompilerParams(vmem_limit_bytes=48 * 1024 * 1024),
        name="lse",
    )(core, scale, *[gathered] * (lots + 1))


STEP = 512


def pull_kernel(core_ref, scale_ref, clip_ref, sums_ref, other_ref, g_ref, h_ref, e_ref, st_ref, q_ref, out_ref, inv_ref, grown_ref):
    core = core_ref[0]
    temper, bound = scale_ref[0], clip_ref[0]
    k = temper * LOG2E
    inv_ref[1:2, :] = 1.0 / (sums_ref[:, 0:ROWS] + other_ref[:, 0:ROWS])
    mine, theirs = 1.0 / sums_ref[:, ROWS:], 1.0 / other_ref[:, ROWS:]
    inv_ref[0:1, 0:HALF] = jnp.where(core == 0, mine, theirs)
    inv_ref[0:1, HALF:] = jnp.where(core == 0, theirs, mine)
    loss = jnp.zeros((BD, 1), f32)
    square = jnp.full((BD, 1), 1e-06, f32)
    grads = []
    step = STEP
    for side in range(2):
        away = 1 - side
        own = h_ref[:, DE * side : DE * (side + 1)]
        total = jnp.zeros((BD, 128), f32)
        for j in range(ROWS // step):
            keys = g_ref[j * step : (j + 1) * step, DE * away : DE * (away + 1)]
            s = lax.dot_general(own, keys, NT, preferred_element_type=f32)
            grown = jnp.exp2(s * k)
            grown_ref[:, j * step : (j + 1) * step] = grown
            total = total + fold_lanes(grown)
        total = jnp.sum(total, axis=1, keepdims=True)
        own_inv = 1.0 / total
        d = jnp.zeros((BD, DE), f32)
        for j in range(ROWS // step):
            keys = g_ref[j * step : (j + 1) * step, DE * away : DE * (away + 1)]
            far = inv_ref[away : away + 1, j * step : (j + 1) * step]
            w = (grown_ref[:, j * step : (j + 1) * step] * (own_inv + far)).astype(bf16)
            d = d + jnp.dot(w, keys, preferred_element_type=f32)
        f_own = own.astype(f32)
        f_away = h_ref[:, DE * away : DE * (away + 1)].astype(f32)
        diag = temper * jnp.sum(f_own * f_away, axis=1, keepdims=True)
        loss = loss + (jnp.log(total) - diag)
        d = temper * d - 2.0 * temper * f_away
        e = e_ref[:, DE * side : DE * (side + 1)]
        inv = st_ref[:, 256 * side : 256 * side + 1]
        size = st_ref[:, 256 * side + 128 : 256 * side + 129]
        grad = (d - e * jnp.sum(e * d, axis=1, keepdims=True)) * inv
        square = square + size * jnp.sum(grad * grad, axis=1, keepdims=True)
        grads.append(grad)
    norm = jnp.sqrt(square)
    factor = jnp.minimum(1.0, bound / norm)
    count = 1.0 / (1.0 + jnp.exp((norm - bound) / (0.1 * bound)))
    for side in range(2):
        q = (factor * grads[side]).T.astype(bf16)
        q_ref[:, PER * side : PER * (side + 1), :] = q.reshape(NPL, PER, BD)
    out_ref[0:1, :] = jnp.broadcast_to(jnp.sum(loss, axis=0, keepdims=True), (1, 128))
    out_ref[1:2, :] = jnp.broadcast_to(jnp.sum(count, axis=0, keepdims=True), (1, 128))
    out_ref[2:8, :] = jnp.zeros((6, 128), f32)


def pull(core, scale, clip_bound, sums, other, gathered, h, e, stats):
    return pl.pallas_call(
        pull_kernel,
        out_shape=(
            jax.ShapeDtypeStruct((NPL, 2 * PER, BD), bf16),
            jax.ShapeDtypeStruct((8, 128), f32),
        ),
        in_specs=[SMEM_SPEC] * 3 + [VMEM_SPEC] * 6,
        out_specs=[VMEM_SPEC] * 2,
        scratch_shapes=[
            pltpu.VMEM((2, ROWS), f32),
            pltpu.VMEM((BD, ROWS), f32),
        ],
        compiler_params=PARAMS,
        name="pull",
    )(core, scale, clip_bound, sums, other, gathered, h, e, stats)


GROUP = 4


def share_kernel(core_ref, q_ref, f_ref, g_ref, part_ref, out_ref, acc_ref):
    core, step = core_ref[0], pl.program_id(0)

    @pl.when(step == 0)
    def _():
        acc_ref[...] = jnp.zeros_like(acc_ref)

    for side, (low, width) in enumerate(((0, DI), (DI, DT))):
        rows = slice(PER * side, PER * (side + 1))
        for ref, which in ((f_ref, core), (g_ref, 1 - core)):
            left = jnp.concatenate([q_ref[NC * p + which, rows, :] for p in range(GROUP)], axis=1)
            right = ref[:, :, low : low + width].reshape(GROUP * BD, width)
            acc_ref[:, low : low + width] += jnp.dot(left, right, preferred_element_type=f32)

    @pl.when(step == NXY // GROUP - 1)
    def _():
        lane = lax.broadcasted_iota(jnp.int32, (1, 128), 1)
        tail = jnp.where(lane < 3, part_ref[0:1, :], jnp.where(lane < 6, part_ref[1:2, :], 0.0))
        for m in range(PER):
            out_ref[m, :, 0:WIDE] = acc_ref[m : m + 1, :]
            out_ref[m, :, WIDE:] = tail


def share(core, q, feats, others, part):
    return pl.pallas_call(
        share_kernel,
        grid_spec=pltpu.PrefetchScalarGridSpec(
            num_scalar_prefetch=1,
            grid=(NXY // GROUP,),
            in_specs=[
                pl.BlockSpec((NC * GROUP, 2 * PER, BD), lambda i, core: (i, 0, 0)),
                pl.BlockSpec((GROUP, BD, WIDE), lambda i, core: (i, 0, 0)),
                pl.BlockSpec((GROUP, BD, WIDE), lambda i, core: (i, 0, 0)),
                pl.BlockSpec((8, 128), lambda i, core: (0, 0)),
            ],
            out_specs=pl.BlockSpec((PER, 1, LONG), lambda i, core: (0, 0, 0)),
            scratch_shapes=[pltpu.VMEM((PER, WIDE), f32)],
        ),
        out_shape=jax.ShapeDtypeStruct((PER, 1, LONG), f32),
        compiler_params=PARAMS,
        name="share",
    )(core, q, feats, others, part)


def finish_kernel(clip_ref, v_ref, noise_ref, out_ref):
    bound = clip_ref[0]
    total = v_ref[0]
    for k in range(1, NZ):
        total = total + v_ref[k]
    grad = (total + bound * noise_ref[...]) / bound
    rest = total[:, WIDE:]
    lane = lax.broadcasted_iota(jnp.int32, (1, 128), 1)
    packed = jnp.zeros((1, 128), f32)
    for n in range(3):
        term = rest.astype(bf16).astype(f32)
        packed = jnp.where((lane == n) | (lane == 3 + n), term, packed)
        rest = rest - term
    rows = [grad[:, 128 * k : 128 * (k + 1)] for k in range(WIDE // 128)] + [packed]
    out = jnp.concatenate(rows + [jnp.zeros((16 - len(rows), 128), f32)], axis=0).astype(bf16)
    for k in range(NZ):
        out_ref[k] = out


def finish(clip_bound, received, noise):
    return pl.pallas_call(
        finish_kernel,
        out_shape=jax.ShapeDtypeStruct((NZ, 16, 128), bf16),
        in_specs=[SMEM_SPEC] + [VMEM_SPEC] * 2,
        out_specs=VMEM_SPEC,
        compiler_params=PARAMS,
        name="finish",
    )(clip_bound, received, noise)


def final_kernel(core_ref, clip_ref, noise_ref, a_ref, b_ref, gi_ref, gt_ref, loss_ref, bound_ref):
    core = core_ref[0]
    mine, theirs = a_ref[...], b_ref[...]
    both = (jnp.where(core == 0, mine, theirs), jnp.where(core == 0, theirs, mine))
    for k in range(WIDE // 128):
        part = slice(128 * k, 128 * (k + 1))
        rows = [both[c][p, :, part] for p in range(NXY) for c in range(NC)]
        block = jnp.concatenate(rows, axis=0).T
        if k < DI // 128:
            gi_ref[part, :] = block
        else:
            gt_ref[128 * k - DI : 128 * (k + 1) - DI, :] = block
    tail = jnp.zeros((NZ, 128), f32)
    for p in range(NXY):
        tail = tail + (both[0][p, :, WIDE:].astype(f32) + both[1][p, :, WIDE:].astype(f32))
    row = tail[0:1, :]
    lane = lax.broadcasted_iota(jnp.int32, (1, 128), 1)
    loss = jnp.sum(jnp.where(lane < 3, row, 0.0), axis=1, keepdims=True)
    count = jnp.sum(jnp.where((lane >= 3) & (lane < 6), row, 0.0), axis=1, keepdims=True)
    frac = (count + 0.05 * BATCH * noise_ref[0]) / BATCH
    bound = clip_ref[0] * jnp.exp(-0.2 * (frac - 0.5))
    loss_ref[0] = jnp.sum(loss / (2.0 * BATCH))
    bound_ref[0] = jnp.sum(bound)


def final(core, clip_bound, noise_count, mine, theirs):
    return pl.pallas_call(
        final_kernel,
        out_shape=(
            jax.ShapeDtypeStruct((DI, DE), bf16),
            jax.ShapeDtypeStruct((DT, DE), bf16),
            jax.ShapeDtypeStruct((1,), f32),
            jax.ShapeDtypeStruct((1,), f32),
        ),
        in_specs=[SMEM_SPEC] * 3 + [VMEM_SPEC] * 2,
        out_specs=[VMEM_SPEC] * 2 + [SMEM_SPEC] * 2,
        compiler_params=PARAMS,
        name="final",
    )(core, clip_bound, noise_count, mine, theirs)


def place(z, xh, xl, y, c):
    return (((z * 2 + xh) * 2 + xl) * 4 + y) * 2 + c


def pairs(target):
    out = []
    for z in range(16):
        for xh in range(2):
            for xl in range(2):
                for y in range(4):
                    for c in range(2):
                        out.append((place(z, xh, xl, y, c), place(*target(z, xh, xl, y, c))))
    return out


REGROUP = pairs(lambda z, xh, xl, y, c: (z, c, xl, y, xh))
CORES = pairs(lambda z, xh, xl, y, c: (z, xh, xl, y, 1 - c))


def noise_column(noise, column):
    part = lax.dynamic_slice(noise, (0, column), (noise.shape[0], 1))
    return part.astype(f32).reshape(1, noise.shape[0])


def local(img_feat, txt_feat, img_proj, txt_proj, logit_scale, clip_bound, noise_img, noise_txt, noise_count):
    z, c = lax.axis_index("z"), lax.axis_index("c")
    at = lax.axis_index(XY)
    core = c.astype(jnp.int32).reshape(1)
    feats = lax.ppermute(jnp.concatenate([img_feat, txt_feat], axis=1), AX, REGROUP)
    h, e, stats = embed(feats, img_proj, txt_proj)
    gathered = lax.all_gather(h, ("z", "c"), axis=0, tiled=True)
    spread = lax.all_to_all(jnp.broadcast_to(feats[None], (NXY, BD, WIDE)), XY, 0, 0)
    beside = lax.ppermute(spread, AX, CORES)
    column = PER * (NC * at + c) + z
    noise = jnp.concatenate(
        [noise_column(noise_img, column), noise_column(noise_txt, column), jnp.zeros((1, 128), f32)], axis=1
    )
    gathered, spread, noise = lax.optimization_barrier((gathered, spread, noise))
    sums = jnp.concatenate(lse_sums(core, logit_scale, gathered), axis=1)
    other = lax.ppermute(sums, AX, CORES)
    q, part = pull(core, logit_scale, clip_bound, sums, other, gathered, h, e, stats)
    q = lax.all_to_all(q, PLANE, 0, 0)
    mine = share(core, q, spread, beside, part)
    mine = finish(clip_bound, lax.all_to_all(mine, "z", 0, 0), noise)
    mine = lax.all_to_all(mine, "z", 0, 0)[:, 0 : LONG // 128, :].reshape(NZ, LONG)
    mine = lax.all_to_all(jnp.broadcast_to(mine[None], (NXY, NZ, LONG)), XY, 0, 0)
    theirs = lax.ppermute(mine, AX, CORES)
    return final(core, clip_bound, noise_count, mine, theirs)


def solution(mesh):
    fine = Mesh(mesh.devices.reshape(DIMS), AX)
    whole = P()
    return jax.shard_map(
        local,
        mesh=fine,
        in_specs=(P(AX, None), P(AX, None)) + (whole,) * 7,
        out_specs=(whole,) * 4,
        check_vma=False,
    )
```
